512 devices in a mesh: dp: 8 (over z), ctx: 64 (over x, y, core).
Axes of the slice: x: 4, y: 8, z: 8, core: 2. Of those that a mesh axis runs over, the one named last changes fastest.
Arguments:
- inputs: bfloat16 [8, 8192, 5120], P('dp', 'ctx'), may hold values from -16 to 16
- queries: bfloat16 [8, 8192, 512], P('dp', 'ctx'), may hold values from -4.5 to 4.5
- key_rows: bfloat16 [8, 8192, 512], P('dp', 'ctx'), may hold values from -4.5 to 4.5
- values: bfloat16 [8, 8192, 512], P('dp', 'ctx'), may hold values from -6 to 6
- frozen_output_gradient: bfloat16 [8, 8192, 512], P('dp', 'ctx'), may hold values from -6 to 6
- out_grad: bfloat16 [8, 8192, 5120], P('dp', 'ctx'), may hold values from -16 to 16
- block_lists: int32 [8, 256, 12], P('dp', 'ctx'), may hold values from -1 to 255, as said below
- down_qkv: bfloat16 [3, 5120, 64], P(None, ('dp', 'ctx')), may hold values from -0.078125 to 0.078125
- up_qkv: bfloat16 [3, 64, 512], replicated, may hold values from -0.75 to 0.75
- output_down_projection: bfloat16 [512, 64], replicated, may hold values from -0.25 to 0.25
- up_out: bfloat16 [64, 5120], P(None, ('dp', 'ctx')), may hold values from -0.078125 to 0.078125
Outputs:
- grad_queries: bfloat16 [8, 8192, 512], P('dp', 'ctx')
- grad_keys: bfloat16 [8, 8192, 512], P('dp', 'ctx')
- grad_values: bfloat16 [8, 8192, 512], P('dp', 'ctx')
- grad_down_qkv: float32 [3, 5120, 64], P(None, ('dp', 'ctx'))
- grad_up_qkv: float32 [3, 64, 512], replicated
- grad_down_out: float32 [512, 64], replicated
- grad_up_out: float32 [64, 5120], P(None, ('dp', 'ctx'))
The draws below stay inside these ranges and needn't reach their ends.
Inputs may be any that keep to these rules, and one draw needn't show every extreme that they name: `block_lists`: row b of a sample lists the 4 blocks of its own frame (frame b // 4), half of 4 distinct blocks of each adjacent frame, and one block of each frame at distance 2 and 3; a slot is -1 where that frame lies outside the video.
All inputs are finite; a program needn't handle non-finite values.
Results may differ from the reference program's by a relative error of at most 0.025.
Values may be sent and summed in bfloat16 or wider, within the bound.
No kernel may reach another device: no remote copies, remote signals or barrier semaphores. Data moves between devices by JAX's collectives and lax.ppermute only.
A program may use at most 64 MiB of HBM per device.

```python
import jax
import jax.numpy as jnp
from jax import lax

D = 5120
HDIM = 128
HEADS = 4
RANK = 64
BLK_DEV = 4
TOK_DEV = 128
SAMPLES = 8
SEQ = 8192
NBLK = 256
BLK = 32
N_CTX = 64


def draw_queries(key, part):
    key = jax.random.fold_in(key, 21)
    result = jnp.clip(jax.random.normal(key, (SAMPLES, SEQ, HEADS * HDIM), jnp.float32), -4.5, 4.5)
    return result.astype(jnp.bfloat16)


def draw_key_rows(key, part):
    key = jax.random.fold_in(key, 37)
    result = jnp.clip(jax.random.normal(key, (SAMPLES, SEQ, HEADS * HDIM), jnp.float32), -4.5, 4.5)
    return result.astype(jnp.bfloat16)


def draw_block_lists(key, part):
    key = jax.random.fold_in(key, 53)
    keys = jax.random.split(key, 6)
    frame_count = NBLK // BLK_DEV
    block = jnp.arange(NBLK, dtype=jnp.int32)
    frame = block // BLK_DEV
    within = jnp.arange(BLK_DEV, dtype=jnp.int32)
    own = jnp.broadcast_to(frame[:, None] * BLK_DEV + within[None, :], (SAMPLES, NBLK, BLK_DEV))
    columns = [own]
    for index, side in enumerate((-1, 1)):
        scores = jax.random.randint(keys[index], (SAMPLES, NBLK, BLK_DEV), 0, 1024) * BLK_DEV + within
        picks = jnp.argsort(scores, axis=-1)[..., :BLK_DEV // 2].astype(jnp.int32)
        target = frame + side
        valid = (target >= 0) & (target < frame_count)
        entry = target[None, :, None] * BLK_DEV + picks
        columns.append(jnp.where(valid[None, :, None], entry, -1))
    for index, side in enumerate((-3, -2, 2, 3)):
        picks = jax.random.randint(keys[2 + index], (SAMPLES, NBLK, 1), 0, BLK_DEV)
        target = frame + side
        valid = (target >= 0) & (target < frame_count)
        entry = target[None, :, None] * BLK_DEV + picks
        columns.append(jnp.where(valid[None, :, None], entry, -1))
    return jnp.concatenate(columns, axis=-1).astype(jnp.int32)


def spiked(values, rng, source, target, parts, factor):
    def block_of(axis_at):
        return (jnp.arange(values.shape[axis_at]) // (values.shape[axis_at] // parts)).reshape((-1,) + (1,) * (values.ndim - 1 - axis_at))

    near = jax.random.permutation(rng, parts)[block_of(target)]
    second = (block_of(target) + parts // 2) % parts
    return jnp.where((block_of(source) == near) | (block_of(source) == second), factor * values, values)


def shard_levels(rng, extent, shards, low, top_value):
    gain = 1.0
    for dim, shards_of in shards:
        draws = jax.random.uniform(jax.random.fold_in(jax.random.fold_in(rng, 6), dim), (shards_of,), jnp.float32, low / len(shards), top_value / len(shards))
        gain = gain * jnp.repeat(jnp.exp(draws), extent[dim] // shards_of).reshape((-1,) + (1,) * (len(extent) - 1 - dim))
    return gain


def noise(rng, dims, deviation, most, cuts=(), kind=jnp.bfloat16):
    drawn = jax.random.normal(rng, dims, jnp.float32) * deviation
    if len(cuts) > 0:
        drawn = shard_levels(rng, dims, cuts, -0.22, 0.18) * drawn
    return jnp.clip(drawn, min=-most, max=most).astype(kind)


def gaussian_with(key, dims, deviation, limit, shards, heavy, kind=jnp.bfloat16):
    drawn = deviation * jax.random.normal(key, dims, jnp.float32)
    if shards:
        drawn = drawn * shard_levels(key, dims, shards, -0.22, 0.18)
    return jnp.clip(spiked(drawn, jax.random.fold_in(key, 3), *heavy), -limit, limit).astype(kind)


def setup_inputs(seed: int = 0) -> dict:
    key_of = jax.random.split(jax.random.key(seed), 12)
    inputs = gaussian_with(key_of[0], (SAMPLES, SEQ, D), 1.0, 16.0, ((0, 8), (1, 64)), (1, 2, 64, 4.0))
    queries = draw_queries(jax.random.fold_in(key_of[11], 71), 0)
    key_rows = draw_key_rows(jax.random.fold_in(key_of[11], 71), 0)
    values = noise(key_of[3], (SAMPLES, SEQ, HEADS * HDIM), 1.0, 6.0, ((0, 8), (1, 64)))
    frozen_output_gradient = noise(key_of[4], (SAMPLES, SEQ, HEADS * HDIM), 1.0, 6.0, ((0, 8), (1, 64)))
    out_grad = gaussian_with(key_of[5], (SAMPLES, SEQ, D), 1.0, 16.0, ((0, 8), (1, 64)), (1, 2, 64, 4.0))
    block_lists = draw_block_lists(jax.random.fold_in(key_of[11], 71), 0)
    down_qkv = noise(key_of[7], (3, D, RANK), D ** -0.5, 0.078125, ((1, 512),))
    up_qkv = noise(key_of[8], (3, RANK, HEADS * HDIM), RANK ** -0.5, 0.75)
    output_down_projection = noise(key_of[9], (HEADS * HDIM, RANK), (HEADS * HDIM) ** -0.5, 0.25)
    up_out = noise(key_of[10], (RANK, D), D ** -0.5, 0.078125, ((1, 512),))
    return {"inputs": inputs, "queries": queries, "key_rows": key_rows, "values": values, "frozen_output_gradient": frozen_output_gradient, "out_grad": out_grad, "block_lists": block_lists, "down_qkv": down_qkv, "up_qkv": up_qkv, "output_down_projection": output_down_projection, "up_out": up_out}


adapter_strength = 2.0
reach_frames = 3


def block_mask(lists, first_block, block_count):
    block_ids = first_block + jnp.arange(block_count, dtype=jnp.int32)
    matched = jnp.any(lists[:, None, :] == block_ids[None, :, None], axis=-1)
    return matched & (block_ids >= 0)[None, :]


def round_trip(array):
    return lax.optimization_barrier(array.astype(jnp.bfloat16)).astype(jnp.float32)


def frame_backward(query_rows, key_window, value_window, grad_rows, allowed):
    count_q = query_rows.shape[0]
    count_k = key_window.shape[0]
    scaling = HDIM ** -0.5
    query_heads = query_rows.astype(jnp.float32).reshape(count_q, HEADS, HDIM)
    key_heads = key_window.astype(jnp.float32).reshape(count_k, HEADS, HDIM)
    value_heads = value_window.astype(jnp.float32).reshape(count_k, HEADS, HDIM)
    grad_heads = grad_rows.astype(jnp.float32).reshape(count_q, HEADS, HDIM)
    scores = jnp.einsum("qhd,khd->hqk", query_heads, key_heads) * scaling
    scores = jnp.where(allowed[None], scores, -jnp.inf)
    highest = jnp.max(scores, axis=-1, keepdims=True)
    log_total = highest + jnp.log(jnp.sum(jnp.exp(scores - highest), axis=-1, keepdims=True))
    probs = jnp.exp(scores - log_total)
    probs_low = round_trip(probs)
    attn = jnp.einsum("hqk,khd->qhd", probs_low, value_heads).reshape(count_q, HEADS * HDIM).astype(jnp.bfloat16)
    attn_wide = lax.optimization_barrier(attn).astype(jnp.float32).reshape(count_q, HEADS, HDIM)
    delta = jnp.sum(grad_heads * attn_wide, axis=-1)
    dprob = jnp.einsum("qhd,khd->hqk", grad_heads, value_heads)
    dscore = round_trip(probs * (dprob - jnp.transpose(delta)[:, :, None]))
    grad_q = (jnp.einsum("hqk,khd->qhd", dscore, key_heads) * scaling).reshape(count_q, HEADS * HDIM)
    grad_k = (jnp.einsum("hqk,qhd->khd", dscore, query_heads) * scaling).reshape(count_k, HEADS * HDIM)
    grad_v = jnp.einsum("hqk,qhd->khd", probs_low, grad_heads).reshape(count_k, HEADS * HDIM)
    return attn, grad_q, grad_k, grad_v


def reference(inputs, queries, key_rows, values, frozen_output_gradient, out_grad, block_lists, down_qkv, up_qkv, output_down_projection, up_out):
    margin = reach_frames * TOK_DEV
    span = (2 * reach_frames + 1) * TOK_DEV

    def one_sample(sample):
        inputs_s, queries_s, keys_s, values_s, base_s, outg_s, lists_s = sample
        output_low_rank = jnp.dot(outg_s, up_out.T, preferred_element_type=jnp.float32).astype(jnp.bfloat16)
        output_gradient_rows = (base_s.astype(jnp.float32) + adapter_strength * jnp.dot(output_low_rank, output_down_projection.T, preferred_element_type=jnp.float32)).astype(jnp.bfloat16)
        key_pad = jnp.pad(keys_s, ((margin, margin), (0, 0)))
        value_pad = jnp.pad(values_s, ((margin, margin), (0, 0)))

        def step(carry, frame):
            dk_pad, dv_pad = carry
            start = frame * TOK_DEV
            query_rows = lax.dynamic_slice_in_dim(queries_s, start, TOK_DEV, 0)
            grad_rows = lax.dynamic_slice_in_dim(output_gradient_rows, start, TOK_DEV, 0)
            key_window = lax.dynamic_slice_in_dim(key_pad, start, span, 0)
            value_window = lax.dynamic_slice_in_dim(value_pad, start, span, 0)
            lists_here = lax.dynamic_slice_in_dim(lists_s, frame * BLK_DEV, BLK_DEV, 0)
            matched = block_mask(lists_here, (frame - reach_frames) * BLK_DEV, (2 * reach_frames + 1) * BLK_DEV)
            allowed = jnp.repeat(jnp.repeat(matched, BLK, 0), BLK, 1)
            attn, grad_q, grad_k, grad_v = frame_backward(query_rows, key_window, value_window, grad_rows, allowed)
            dk_pad = lax.dynamic_update_slice_in_dim(dk_pad, lax.dynamic_slice_in_dim(dk_pad, start, span, 0) + grad_k, start, 0)
            dv_pad = lax.dynamic_update_slice_in_dim(dv_pad, lax.dynamic_slice_in_dim(dv_pad, start, span, 0) + grad_v, start, 0)
            return (dk_pad, dv_pad), (attn, grad_q)

        zeros = jnp.zeros((SEQ + 2 * margin, HEADS * HDIM), jnp.float32)
        (dk_pad, dv_pad), (attn, grad_q) = lax.scan(step, (zeros, zeros), jnp.arange(N_CTX, dtype=jnp.int32))
        attn = attn.reshape(SEQ, HEADS * HDIM)
        grad_q = grad_q.reshape(SEQ, HEADS * HDIM).astype(jnp.bfloat16)
        grad_k = dk_pad[margin:margin + SEQ].astype(jnp.bfloat16)
        grad_v = dv_pad[margin:margin + SEQ].astype(jnp.bfloat16)
        grads = (grad_q, grad_k, grad_v)
        up_terms = []
        down_terms = []
        for index in range(3):
            low_in = jnp.dot(inputs_s, down_qkv[index], preferred_element_type=jnp.float32).astype(jnp.bfloat16)
            up_terms.append(jnp.dot(low_in.T, grads[index], preferred_element_type=jnp.float32))
            factor = jnp.dot(grads[index], up_qkv[index].T, preferred_element_type=jnp.float32).astype(jnp.bfloat16)
            down_terms.append(jnp.dot(inputs_s.T, factor, preferred_element_type=jnp.float32))
        low_attn = jnp.dot(attn, output_down_projection, preferred_element_type=jnp.float32).astype(jnp.bfloat16)
        term_up_out = jnp.dot(low_attn.T, outg_s, preferred_element_type=jnp.float32)
        term_down_out = jnp.dot(attn.T, output_low_rank, preferred_element_type=jnp.float32)
        return grad_q, grad_k, grad_v, jnp.stack(down_terms), jnp.stack(up_terms), term_down_out, term_up_out

    results = lax.map(one_sample, (inputs, queries, key_rows, values, frozen_output_gradient, out_grad, block_lists))
    grad_scale = adapter_strength / (SAMPLES * SEQ) ** 0.5
    grad_down_qkv = jnp.sum(results[3], axis=0) * grad_scale
    grad_up_qkv = jnp.sum(results[4], axis=0) * grad_scale
    grad_down_out = jnp.sum(results[5], axis=0) * grad_scale
    grad_up_out = jnp.sum(results[6], axis=0) * grad_scale
    return (results[0], results[1], results[2], grad_down_qkv, grad_up_qkv, grad_down_out, grad_up_out)
```

```python
import math

import jax
import jax.numpy as jnp
from jax import lax
from jax.experimental import pallas as pl
from jax.experimental.pallas import tpu as pltpu
from jax.sharding import Mesh, PartitionSpec as P

HDIM = 128
BLK = 32
BLK_DEV = 4
NX, NY, NZ = 4, 8, 8
STRENGTH = 2.0
SCALING = HDIM**-0.5
MASKED = -1e30
BF = jnp.bfloat16
F32 = jnp.float32

SEGMENTS = ((0, 128), (128, 384), (384, 640), (640, 896), (896, 1024))


def dot(a, b, ca, cb):
    return lax.dot_general(a, b, (((ca,), (cb,)), ((), ())), preferred_element_type=F32)


def attention_kernel(
    q_ref, l2_ref, l1_ref, own_ref, r1_ref, r2_ref, fog_ref, low_ref, odp_ref, bias_ref,
    attn_ref, dq_ref, pl2_ref, pl1_ref, pown_ref, pr1_ref, pr2_ref,
):
    kv_refs = (l2_ref, l1_ref, own_ref, r1_ref, r2_ref)
    part_refs = (pl2_ref, pl1_ref, pown_ref, pr1_ref, pr2_ref)
    half = q_ref.shape[1]
    dout = (fog_ref[...].astype(F32) + STRENGTH * dot(low_ref[...], odp_ref[...], 1, 1)).astype(BF)
    bias = bias_ref[...]
    for head in range(half // HDIM):
        cols = slice(head * HDIM, (head + 1) * HDIM)
        vcols = slice(half + head * HDIM, half + (head + 1) * HDIM)
        q = q_ref[:, cols]
        dout_h = dout[:, cols]
        keys = [ref[:, cols] for ref in kv_refs]
        vals = [ref[:, vcols] for ref in kv_refs]
        scores = []
        for k, (a, b) in zip(keys, SEGMENTS):
            s = dot(q, k, 1, 1) * SCALING
            s = s.reshape(8, BLK, b - a) + bias[:, None, a:b]
            scores.append(s.reshape(8 * BLK, b - a))
        top = scores[0].max(axis=1, keepdims=True)
        for s in scores[1:]:
            top = jnp.maximum(top, s.max(axis=1, keepdims=True))
        weights = [jnp.exp(s - top) for s in scores]
        total = weights[0].sum(axis=1, keepdims=True)
        for w in weights[1:]:
            total = total + w.sum(axis=1, keepdims=True)
        inverse = 1.0 / total
        probs = [w * inverse for w in weights]
        probs_low = [p.astype(BF) for p in probs]
        attn = dot(probs_low[0], vals[0], 1, 0)
        for p, v in zip(probs_low[1:], vals[1:]):
            attn = attn + dot(p, v, 1, 0)
        attn = attn.astype(BF)
        attn_ref[:, cols] = attn
        delta = (dout_h.astype(F32) * attn.astype(F32)).sum(axis=1, keepdims=True)
        dq = None
        for k, v, p, p_low, out in zip(keys, vals, probs, probs_low, part_refs):
            dscore = (p * (dot(dout_h, v, 1, 1) - delta)).astype(BF)
            term = dot(dscore, k, 1, 0)
            dq = term if dq is None else dq + term
            out[:, cols] = (dot(dscore, q, 0, 0) * SCALING).astype(out.dtype)
            out[:, vcols] = dot(p_low, dout_h, 0, 0).astype(out.dtype)
        dq_ref[:, cols] = (dq * SCALING).astype(BF)


def attention(q, windows, fog, low_out, odp_half, bias):
    rows, half = q.shape
    shape = jax.ShapeDtypeStruct
    outs = [shape((rows, half), BF), shape((rows, half), BF)]
    outs += [shape((b - a, 2 * half), F32 if i == 2 else BF) for i, (a, b) in enumerate(SEGMENTS)]
    vmem = pl.BlockSpec(memory_space=pltpu.VMEM)
    return pl.pallas_call(
        attention_kernel,
        out_shape=outs,
        in_specs=[vmem] * 10,
        out_specs=[vmem] * 7,
        compiler_params=pltpu.CompilerParams(vmem_limit_bytes=40 * 1024 * 1024),
        cost_estimate=pl.CostEstimate(flops=1_400_000_000, bytes_accessed=4_000_000, transcendentals=524288),
        name="attention",
    )(q, *windows, fog, low_out, odp_half, bias)


def exchange(parts, axes):
    return lax.all_to_all(parts, axes, split_axis=0, concat_axis=0, tiled=True)


def spread(block, axes, peers):
    return exchange(jnp.broadcast_to(block[None], (peers,) + block.shape), axes)


def swap(block):
    return lax.ppermute(block, "c", [(0, 1), (1, 0)])


def chip_shift(block, by):
    chips = NX * NY
    return lax.ppermute(block, ("x", "y"), [(i, i + by) for i in range(chips) if 0 <= i + by < chips])


def shards(
    inputs, queries, key_rows, values, frozen_output_gradient, out_grad, block_lists,
    down_qkv, up_qkv, output_down_projection, up_out,
):
    x_own, y_own = inputs[0], out_grad[0]
    rows, feats = queries.shape[1:]
    half = feats // 2
    rank = output_down_projection.shape[1]
    width = x_own.shape[1]
    own_cols = down_qkv.shape[1]
    core = lax.axis_index("c")
    first = core == 0
    chip = lax.axis_index("x") * NY + lax.axis_index("y")
    grad_scale = STRENGTH / math.sqrt(NX * NY * NZ * 2 * rows)

    lists = jnp.pad(block_lists[0].astype(BF), ((0, 12), (0, half - block_lists.shape[2])))
    stack = jnp.concatenate([queries[0], frozen_output_gradient[0], key_rows[0], values[0]], axis=0)
    stack = jnp.stack([stack[:, :half], stack[:, half:]])
    stack = jnp.concatenate([stack, jnp.broadcast_to(lists[None], (2,) + lists.shape)], axis=1)
    chip_stack = exchange(stack, "c")
    q_chip = chip_stack[:, :rows].reshape(2 * rows, half)
    fog_chip = chip_stack[:, rows : 2 * rows].reshape(2 * rows, half)
    kv_chip = jnp.concatenate(
        [chip_stack[:, 2 * rows : 3 * rows], chip_stack[:, 3 * rows : 4 * rows]], axis=2
    ).reshape(2 * rows, 2 * half)
    lists_chip = chip_stack[:, 4 * rows : 4 * rows + BLK_DEV, : block_lists.shape[2]].reshape(
        2 * BLK_DEV, -1
    )
    windows = (
        chip_shift(kv_chip[rows:], 2),
        chip_shift(kv_chip, 1),
        kv_chip,
        chip_shift(kv_chip, -1),
        chip_shift(kv_chip[:rows], -2),
    )
    ids = (2 * chip - 3) * BLK_DEV + jnp.arange(8 * BLK_DEV, dtype=jnp.int32)
    allowed = jnp.any(lists_chip[:, :, None] == ids.astype(F32)[None, None, :], axis=1) & (ids >= 0)[None]
    bias = jnp.repeat(jnp.where(allowed, 0.0, MASKED).astype(F32), BLK, axis=1)

    x_other = swap(x_own)
    y_other = lax.ppermute(y_own, "c", [(0, 1)])
    a_own = jnp.where(first, x_own, y_own)
    a_other = jnp.where(first, x_other, y_other)

    shard = jnp.concatenate([down_qkv[0], down_qkv[1], up_out.T, down_qkv[2]], axis=1)
    line = spread(shard.reshape(2, -1), ("y", "c"), 2 * NY).reshape(2 * NY * own_cols, 4 * rank)
    line = lax.dynamic_slice_in_dim(line, core * 2 * rank, 2 * rank, 1)
    plane = spread(line, "z", NZ)
    whole = spread(plane, "x", NX)
    weights = jnp.transpose(whole, (1, 0, 2, 3)).reshape(width, 2 * rank)
    w_a, w_b = weights[:, :rank], weights[:, rank:]
    low_a = jnp.concatenate([dot(a_own, w_a, 1, 0), dot(a_other, w_a, 1, 0)], axis=0).astype(BF)
    low_b = jnp.concatenate([dot(x_own, w_b, 1, 0), dot(x_other, w_b, 1, 0)], axis=0).astype(BF)

    def ordered(pair):
        return jnp.where(first, pair, jnp.concatenate([pair[rows:], pair[:rows]], axis=0))

    low_a, low_b = ordered(low_a), ordered(low_b)
    low_out = jnp.where(first, lax.ppermute(low_a, "c", [(1, 0)]), low_a)
    odp_half = lax.dynamic_slice_in_dim(output_down_projection, core * half, half, 0)

    attn, dq, p_l2, p_l1, p_own, p_r1, p_r2 = attention(q_chip, windows, fog_chip, low_out, odp_half, bias)
    from_r2 = chip_shift(p_l2, -2)
    from_r1 = chip_shift(p_l1, -1)
    from_l1 = chip_shift(p_r1, 1)
    from_l2 = chip_shift(p_r2, 2)

    m_a = jnp.where(first, up_qkv[0].T, output_down_projection)
    m_b = jnp.where(first, up_qkv[1].T, up_qkv[2].T)

    def halves(matrix):
        mine = lax.dynamic_slice_in_dim(matrix, core * half, half, 0)
        theirs = lax.dynamic_slice_in_dim(matrix, (1 - core) * half, half, 0)
        return mine, theirs

    def role(kept, got, low, matrix):
        mine, theirs = halves(matrix)
        factor = (dot(kept, mine, 1, 0) + dot(got, theirs, 1, 0)).astype(BF)
        left = jnp.where(first, kept, got)
        right = jnp.where(first, got, kept)
        up = dot(low, jnp.concatenate([left, right], axis=1), 0, 0)
        return factor, up

    got_a = swap(jnp.where(first, attn, dq))
    kept_a = jnp.where(first, dq, attn)
    factor_a, up_a = role(kept_a, got_a, low_a, m_a)

    total = p_own + from_r1.astype(F32) + from_l1.astype(F32)
    total = total + jnp.concatenate([from_l2, from_r2], axis=0).astype(F32)
    total = total.astype(BF)
    dk, dv = total[:, :half], total[:, half:]
    got_b = swap(jnp.where(first, dv, dk))
    kept_b = jnp.where(first, dk, dv)
    factor_b, up_b = role(kept_b, got_b, low_b, m_b)

    def mine_first(pair):
        own = lax.dynamic_slice_in_dim(pair, core * rows, rows, 0)
        other = lax.dynamic_slice_in_dim(pair, (1 - core) * rows, rows, 0)
        return own, other

    fa_own, fa_other = mine_first(factor_a)
    fb_own, fb_other = mine_first(factor_b)
    g_a = dot(a_own, fa_own, 0, 0) + dot(a_other, fa_other, 0, 0)
    g_b = dot(x_own, fb_own, 0, 0) + dot(x_other, fb_other, 0, 0)
    g = (jnp.concatenate([g_a, g_b], axis=1) * grad_scale).astype(BF)
    line_rows = 2 * NY * own_cols
    g = jnp.transpose(g.reshape(NZ, NX, line_rows, 2 * rank), (1, 0, 2, 3))
    u_rows = 2 * rank * feats // (NX * NZ * 2 * rank)
    u = (jnp.concatenate([up_a, up_b], axis=0) * grad_scale).astype(BF)
    u = u.reshape(NX, NZ, u_rows, 2 * rank)
    step = exchange(jnp.concatenate([g, u], axis=2), "x")
    step = step.astype(F32).sum(axis=0).astype(BF)
    step = exchange(step, "z")
    step = step.astype(F32).sum(axis=0).astype(BF)
    g_line = step[:line_rows].reshape(2 * NY, own_cols, 2 * rank)
    u_line = jnp.broadcast_to(step[line_rows:][None], (2 * NY, u_rows, 2 * rank))
    step = exchange(jnp.concatenate([g_line, u_line], axis=1), ("y", "c"))
    step = step.reshape(NY, 2, own_cols + u_rows, 2 * rank).astype(F32).sum(axis=0)
    g_out = step[:, :own_cols]
    grad_down = jnp.stack([g_out[0, :, :rank], g_out[0, :, rank:], g_out[1, :, rank:]])
    grad_up_out = g_out[1, :, :rank].T
    u_all = spread(spread(step[:, own_cols:].astype(BF), "z", NZ), "x", NX)
    u_all = jnp.transpose(u_all, (2, 0, 1, 3, 4)).reshape(2, 2, rank, feats).astype(F32)
    grad_up = jnp.stack([u_all[0, 0], u_all[0, 1], u_all[1, 1]])
    grad_down_out = u_all[1, 0].T

    result = jnp.concatenate([dq, dk, dv], axis=1).reshape(2, rows, 3 * half)
    result = exchange(result, "c")
    grad_q, grad_k, grad_v = (
        jnp.concatenate([result[0, :, i * half : (i + 1) * half], result[1, :, i * half : (i + 1) * half]], axis=1)
        for i in range(3)
    )
    return grad_q[None], grad_k[None], grad_v[None], grad_down, grad_up, grad_down_out, grad_up_out


def solution(mesh):
    fine = Mesh(mesh.devices.reshape(NZ, NX, NY, 2), ("z", "x", "y", "c"))
    ctx = ("x", "y", "c")
    every = ("z", "x", "y", "c")
    tokens = P("z", ctx, None)
    return jax.shard_map(
        shards,
        mesh=fine,
        in_specs=(tokens,) * 7 + (P(None, every, None), P(), P(), P(None, every)),
        out_specs=(tokens,) * 3 + (P(None, every, None), P(), P(), P(None, every)),
        check_vma=False,
    )
```

```python
import math

import jax
import jax.numpy as jnp
from jax import lax
from jax.experimental import pallas as pl
from jax.experimental.pallas import tpu as pltpu
from jax.sharding import Mesh, PartitionSpec as P

HDIM = 128
BLK = 32
BLK_DEV = 4
NX, NY, NZ = 4, 8, 8
STRENGTH = 2.0
SCALING = HDIM**-0.5
MASKED = -1e30
BF = jnp.bfloat16
F32 = jnp.float32

SEGMENTS = ((0, 128), (128, 384), (384, 640), (640, 896), (896, 1024))


def dot(a, b, ca, cb):
    return lax.dot_general(a, b, (((ca,), (cb,)), ((), ())), preferred_element_type=F32)


def attention_kernel(
    core_ref, q_ref, l2_ref, l1_ref, own_ref, r1_ref, r2_ref, fog_ref, low_ref, odp_ref, bias_ref,
    kept_ref, send_ref, dq_ref, pl2_ref, pl1_ref, pown_ref, pr1_ref, pr2_ref, attn_ref,
):
    kv_refs = (l2_ref, l1_ref, own_ref, r1_ref, r2_ref)
    part_refs = (pl2_ref, pl1_ref, pown_ref, pr1_ref, pr2_ref)
    rows, half = q_ref.shape
    low_out = low_ref[1][:, : odp_ref.shape[1]]
    dout = (fog_ref[...].astype(F32) + STRENGTH * dot(low_out, odp_ref[...], 1, 1)).astype(BF)
    bias = bias_ref[...]
    for head in range(half // HDIM):
        cols = slice(head * HDIM, (head + 1) * HDIM)
        vcols = slice(half + head * HDIM, half + (head + 1) * HDIM)
        q = q_ref[:, cols]
        dout_h = dout[:, cols]
        keys = [ref[:, cols] for ref in kv_refs]
        vals = [ref[:, vcols] for ref in kv_refs]
        scores = []
        for k, (a, b) in zip(keys, SEGMENTS):
            s = dot(q, k, 1, 1) * SCALING
            s = s.reshape(8, BLK, b - a) + bias[:, None, a:b]
            scores.append(s.reshape(8 * BLK, b - a))
        top = scores[0].max(axis=1, keepdims=True)
        for s in scores[1:]:
            top = jnp.maximum(top, s.max(axis=1, keepdims=True))
        weights = [jnp.exp(s - top) for s in scores]
        total = weights[0].sum(axis=1, keepdims=True)
        for w in weights[1:]:
            total = total + w.sum(axis=1, keepdims=True)
        inverse = 1.0 / total
        probs = [w * inverse for w in weights]
        probs_low = [p.astype(BF) for p in probs]
        attn = dot(probs_low[0], vals[0], 1, 0)
        for p, v in zip(probs_low[1:], vals[1:]):
            attn = attn + dot(p, v, 1, 0)
        attn = attn.astype(BF)
        attn_ref[:, cols] = attn
        delta = (dout_h.astype(F32) * attn.astype(F32)).sum(axis=1, keepdims=True)
        dq = None
        for k, v, p, p_low, out in zip(keys, vals, probs, probs_low, part_refs):
            dscore = (p * (dot(dout_h, v, 1, 1) - delta)).astype(BF)
            term = dot(dscore, k, 1, 0)
            dq = term if dq is None else dq + term
            out[:, cols] = (dot(dscore, q, 0, 0) * SCALING).astype(out.dtype)
            out[:, vcols] = dot(p_low, dout_h, 0, 0).astype(out.dtype)
        dq_ref[:, cols] = (dq * SCALING).astype(BF)

    @pl.when(core_ref[0] == 0)
    def _():
        kept_ref[...] = dq_ref[...]
        send_ref[:rows] = attn_ref[...]

    @pl.when(core_ref[0] != 0)
    def _():
        kept_ref[...] = attn_ref[...]
        send_ref[:rows] = dq_ref[...]

    send_ref[rows:] = dq_ref[rows // 2 :]


def attention(core, q, windows, fog, low, odp_half, bias):
    rows, half = q.shape
    shape = jax.ShapeDtypeStruct
    outs = [shape((rows, half), BF), shape((rows + rows // 2, half), BF), shape((rows, half), BF)]
    outs += [shape((b - a, 2 * half), F32 if i == 2 else BF) for i, (a, b) in enumerate(SEGMENTS)]
    vmem = pl.BlockSpec(memory_space=pltpu.VMEM)
    return pl.pallas_call(
        attention_kernel,
        out_shape=outs,
        in_specs=[pl.BlockSpec(memory_space=pltpu.SMEM)] + [vmem] * 10,
        out_specs=[vmem] * 8,
        scratch_shapes=[pltpu.VMEM((rows, half), BF)],
        compiler_params=pltpu.CompilerParams(vmem_limit_bytes=40 * 1024 * 1024),
        cost_estimate=pl.CostEstimate(flops=1_400_000_000, bytes_accessed=4_000_000, transcendentals=524288),
        name="attention",
    )(core, q, *windows, fog, low, odp_half, bias)


Z_STEP = 2


def low_kernel(core_ref, xo_ref, xt_ref, yo_ref, yt_ref, w_ref, low_ref, own_acc, other_acc):
    core = core_ref[0]
    step = pl.program_id(0)
    rows = xo_ref.shape[0]
    ranks = w_ref.shape[3]
    block = NX * w_ref.shape[2]

    @pl.when(step == 0)
    def _():
        own_acc[...] = jnp.zeros_like(own_acc)
        other_acc[...] = jnp.zeros_like(other_acc)

    lane = lax.broadcasted_iota(jnp.int32, (rows, ranks), 1)
    from_y = (lane < ranks // 2) & (core == 1)
    for zz in range(Z_STEP):
        cols = slice(zz * block, (zz + 1) * block)
        w = jnp.concatenate([w_ref[i, zz] for i in range(NX)], axis=0)
        for x_ref, y_ref, acc in ((xo_ref, yo_ref, own_acc), (xt_ref, yt_ref, other_acc)):
            acc[...] += jnp.where(from_y, dot(y_ref[:, cols], w, 1, 0), dot(x_ref[:, cols], w, 1, 0))

    @pl.when(step == pl.num_programs(0) - 1)
    def _():
        low_ref[pl.ds(pl.multiple_of(core * rows, rows), rows)] = own_acc[...].astype(BF)
        low_ref[pl.ds(pl.multiple_of((1 - core) * rows, rows), rows)] = other_acc[...].astype(BF)


def low_factors(core, x_own, x_other, y_own, y_other, weights):
    rows, width = x_own.shape
    pieces, ranks = weights.shape[2:]
    wide = pl.BlockSpec((rows, width * Z_STEP // NZ), lambda i: (0, i))
    return pl.pallas_call(
        low_kernel,
        grid=(NZ // Z_STEP,),
        out_shape=jax.ShapeDtypeStruct((2 * rows, ranks), BF),
        in_specs=[pl.BlockSpec(memory_space=pltpu.SMEM)] + [wide] * 4
        + [pl.BlockSpec((NX, Z_STEP, pieces, ranks), lambda i: (0, i, 0, 0))],
        out_specs=pl.BlockSpec((2 * rows, ranks), lambda i: (0, 0)),
        scratch_shapes=[pltpu.VMEM((rows, ranks), F32), pltpu.VMEM((rows, ranks), F32)],
        compiler_params=pltpu.CompilerParams(vmem_limit_bytes=24 * 1024 * 1024),
        cost_estimate=pl.CostEstimate(flops=700_000_000, bytes_accessed=6_600_000, transcendentals=0),
        name="low_factors",
    )(core, x_own, x_other, y_own, y_other, weights)


def grad_kernel(
    scale, core_ref, xo_ref, xt_ref, yo_ref, yt_ref, kept_a_ref, got_a_ref, kept_b_ref, got_b_ref, low_ref,
    m_a_ref, m_b_ref, g_ref, f_ref, u_ref,
):
    core = core_ref[0]
    step = pl.program_id(0)
    rows = xo_ref.shape[0]
    half = kept_a_ref.shape[1]
    rank = m_a_ref.shape[1]
    block = xo_ref.shape[1] // Z_STEP
    piece = block // NX
    extra = g_ref.shape[2] - piece
    mine = pl.ds(pl.multiple_of(core * half, half), half)
    theirs = pl.ds(pl.multiple_of((1 - core) * half, half), half)

    @pl.when(step == 0)
    def _():
        for i, (kept_ref, got_ref, m_ref) in enumerate(
            ((kept_a_ref, got_a_ref, m_a_ref), (kept_b_ref, got_b_ref, m_b_ref))
        ):
            kept, got = kept_ref[...], got_ref[: 2 * rows]
            ranks = slice(i * rank, (i + 1) * rank)
            low = low_ref[:, ranks]
            f_ref[:, ranks] = (dot(kept, m_ref[mine], 1, 0) + dot(got, m_ref[theirs], 1, 0)).astype(BF)
            u_ref[ranks, mine] = (dot(low, kept, 0, 0) * scale).astype(BF)
            u_ref[ranks, theirs] = (dot(low, got, 0, 0) * scale).astype(BF)

    f_own = f_ref[pl.ds(pl.multiple_of(core * rows, rows), rows)]
    f_other = f_ref[pl.ds(pl.multiple_of((1 - core) * rows, rows), rows)]
    line = lax.broadcasted_iota(jnp.int32, (2 * rank, block), 0)
    from_y = (line < rank) & (core == 1)
    for zz in range(Z_STEP):
        cols = slice(zz * block, (zz + 1) * block)
        gx = dot(f_own, xo_ref[:, cols], 0, 0) + dot(f_other, xt_ref[:, cols], 0, 0)
        gy = dot(f_own, yo_ref[:, cols], 0, 0) + dot(f_other, yt_ref[:, cols], 0, 0)
        g = (jnp.where(from_y, gy, gx) * scale).T.astype(BF)
        at = pl.ds(pl.multiple_of((step * Z_STEP + zz) * extra, extra), extra)
        for i in range(NX):
            g_ref[i, zz, :piece] = g[i * piece : (i + 1) * piece]
            g_ref[i, zz, piece:] = u_ref[at, i * 2 * rank : (i + 1) * 2 * rank]


def grad_partials(scale, core, x_own, x_other, y_own, y_other, kept_a, got_a, kept_b, got_b, low, m_a, m_b):
    rows, width = x_own.shape
    feats, rank = m_a.shape
    piece = width // (NX * NZ)
    extra = 2 * rank // NZ
    wide = pl.BlockSpec((rows, width * Z_STEP // NZ), lambda i: (0, i))
    whole = [pl.BlockSpec(a.shape, lambda i: (0, 0)) for a in (kept_a, got_a, kept_b, got_b, low, m_a, m_b)]
    return pl.pallas_call(
        lambda *refs: grad_kernel(scale, *refs),
        grid=(NZ // Z_STEP,),
        out_shape=jax.ShapeDtypeStruct((NX, NZ, piece + extra, 2 * rank), BF),
        in_specs=[pl.BlockSpec(memory_space=pltpu.SMEM)] + [wide] * 4 + whole,
        out_specs=pl.BlockSpec((NX, Z_STEP, piece + extra, 2 * rank), lambda i: (0, i, 0, 0)),
        scratch_shapes=[pltpu.VMEM((2 * rows, 2 * rank), BF), pltpu.VMEM((2 * rank, feats), BF)],
        compiler_params=pltpu.CompilerParams(vmem_limit_bytes=24 * 1024 * 1024),
        cost_estimate=pl.CostEstimate(flops=800_000_000, bytes_accessed=7_500_000, transcendentals=0),
        name="grad_partials",
    )(core, x_own, x_other, y_own, y_other, kept_a, got_a, kept_b, got_b, low, m_a, m_b)


def exchange(parts, axes):
    return lax.all_to_all(parts, axes, split_axis=0, concat_axis=0, tiled=True)


def spread(block, axes, peers):
    return exchange(jnp.broadcast_to(block[None], (peers,) + block.shape), axes)


def swap(block):
    return lax.ppermute(block, "c", [(0, 1), (1, 0)])


def chip_shift(block, by):
    chips = NX * NY
    return lax.ppermute(block, ("x", "y"), [(i, i + by) for i in range(chips) if 0 <= i + by < chips])


def shards(
    inputs, queries, key_rows, values, frozen_output_gradient, out_grad, block_lists,
    down_qkv, up_qkv, output_down_projection, up_out,
):
    x_own, y_own = inputs[0], out_grad[0]
    rows, feats = queries.shape[1:]
    half = feats // 2
    rank = output_down_projection.shape[1]
    width = x_own.shape[1]
    own_cols = down_qkv.shape[1]
    core = lax.axis_index("c")
    first = core == 0
    chip = lax.axis_index("x") * NY + lax.axis_index("y")
    grad_scale = STRENGTH / math.sqrt(NX * NY * NZ * 2 * rows)

    core_id = core.astype(jnp.int32).reshape(1)

    shard = jnp.concatenate([down_qkv[0], down_qkv[1], up_out.T, down_qkv[2]], axis=1)
    line = spread(shard.reshape(2, -1), ("y", "c"), 2 * NY).reshape(2 * NY * own_cols, 4 * rank)
    line = lax.dynamic_slice_in_dim(line, core * 2 * rank, 2 * rank, 1)

    lists = jnp.pad(block_lists[0].astype(BF), ((0, 12), (0, half - block_lists.shape[2])))
    stack = jnp.concatenate([queries[0], frozen_output_gradient[0], key_rows[0], values[0]], axis=0)
    kept = jnp.concatenate([jnp.where(first, stack[:, :half], stack[:, half:]), lists], axis=0)
    got = swap(jnp.concatenate([jnp.where(first, stack[:, half:], stack[:, :half]), lists], axis=0))
    chip_stack = jnp.stack([jnp.where(first, kept, got), jnp.where(first, got, kept)])
    x_other = swap(x_own)
    y_other = lax.ppermute(y_own, "c", [(0, 1)])
    line, chip_stack, x_other, y_other = lax.optimization_barrier((line, chip_stack, x_other, y_other))

    q_chip = chip_stack[:, :rows].reshape(2 * rows, half)
    fog_chip = chip_stack[:, rows : 2 * rows].reshape(2 * rows, half)
    kv_chip = jnp.concatenate(
        [chip_stack[:, 2 * rows : 3 * rows], chip_stack[:, 3 * rows : 4 * rows]], axis=2
    ).reshape(2 * rows, 2 * half)
    lists_chip = chip_stack[:, 4 * rows : 4 * rows + BLK_DEV, : block_lists.shape[2]].reshape(
        2 * BLK_DEV, -1
    )
    windows = (
        chip_shift(kv_chip[rows:], 2),
        chip_shift(kv_chip, 1),
        kv_chip,
        chip_shift(kv_chip, -1),
        chip_shift(kv_chip[:rows], -2),
    )
    ids = (2 * chip - 3) * BLK_DEV + jnp.arange(8 * BLK_DEV, dtype=jnp.int32)
    allowed = jnp.any(lists_chip[:, :, None] == ids.astype(F32)[None, None, :], axis=1) & (ids >= 0)[None]
    bias = jnp.repeat(jnp.where(allowed, 0.0, MASKED).astype(F32), BLK, axis=1)

    plane = spread(line, "z", NZ)
    weights = spread(plane.reshape(-1, 2 * rank), "x", NX).reshape(NX, NZ, -1, 2 * rank)
    low = low_factors(core_id, x_own, x_other, y_own, y_other, weights)
    low_both = lax.all_gather(low, "c")
    odp_half = lax.dynamic_slice_in_dim(output_down_projection, core * half, half, 0)

    kept_a, send_a, dq, p_l2, p_l1, p_own, p_r1, p_r2 = attention(
        core_id, q_chip, windows, fog_chip, low_both, odp_half, bias
    )
    from_r1 = chip_shift(p_l1, -1)
    from_l1 = chip_shift(p_r1, 1)
    from_r2 = chip_shift(p_l2, -2)
    from_l2 = chip_shift(p_r2, 2)
    got_a = swap(send_a)
    m_a = jnp.where(first, up_qkv[0].T, output_down_projection)
    m_b = jnp.where(first, up_qkv[1].T, up_qkv[2].T)

    total = p_own + from_r1.astype(F32) + from_l1.astype(F32)
    total = total + jnp.concatenate([from_l2, from_r2], axis=0).astype(F32)
    total = total.astype(BF)
    dk, dv = total[:, :half], total[:, half:]
    kept_b = jnp.where(first, dk, dv)
    got_b = swap(
        jnp.concatenate([jnp.where(first, dv, dk), jnp.where(first, dk[rows:], dv[:rows])], axis=0)
    )
    g = grad_partials(
        grad_scale, core_id, x_own, x_other, y_own, y_other, kept_a, got_a, kept_b, got_b, low, m_a, m_b
    )

    line_rows = 2 * NY * own_cols
    u_rows = g.shape[2] - line_rows
    step = exchange(g.reshape(NX, -1, 2 * rank), "x")
    step = step.astype(F32).sum(axis=0).astype(BF).reshape(NZ, -1, 2 * rank)
    step = exchange(step, "z")
    step = step.astype(F32).sum(axis=0).astype(BF)
    g_line = step[:line_rows].reshape(2 * NY, own_cols, 2 * rank)
    u_line = jnp.broadcast_to(step[line_rows:][None], (2 * NY, u_rows, 2 * rank))
    step = exchange(jnp.concatenate([g_line, u_line], axis=1), ("y", "c"))
    step = step.reshape(NY, 2, own_cols + u_rows, 2 * rank).astype(F32).sum(axis=0)
    g_out = step[:, :own_cols]
    grad_down = jnp.stack([g_out[0, :, :rank], g_out[0, :, rank:], g_out[1, :, rank:]])
    grad_up_out = g_out[1, :, :rank].T
    u_mine = step[:, own_cols:].astype(BF).reshape(2 * u_rows, 2 * rank)
    u_all = spread(u_mine, ("x", "z"), NX * NZ).reshape(NX, NZ, 2, u_rows, 2 * rank)
    u_all = jnp.transpose(u_all, (2, 1, 3, 0, 4)).reshape(2, 2, rank, feats).astype(F32)
    grad_up = jnp.stack([u_all[0, 0], u_all[0, 1], u_all[1, 1]])
    grad_down_out = u_all[1, 0].T

    def own_frame(mine, from_zero, from_one):
        left = jnp.where(first, mine[:rows], from_zero)
        right = jnp.where(first, from_one, mine[rows:])
        return jnp.concatenate([left, right], axis=1)[None]

    grad_q = own_frame(dq, got_a[2 * rows :], got_a[:rows])
    grad_k = own_frame(dk, got_b[2 * rows :], got_b[:rows])
    grad_v = own_frame(dv, got_b[rows : 2 * rows], got_b[2 * rows :])
    return grad_q, grad_k, grad_v, grad_down, grad_up, grad_down_out, grad_up_out


def solution(mesh):
    fine = Mesh(mesh.devices.reshape(NZ, NX, NY, 2), ("z", "x", "y", "c"))
    ctx = ("x", "y", "c")
    every = ("z", "x", "y", "c")
    tokens = P("z", ctx, None)
    return jax.shard_map(
        shards,
        mesh=fine,
        in_specs=(tokens,) * 7 + (P(None, every, None), P(), P(), P(None, every)),
        out_specs=(tokens,) * 3 + (P(None, every, None), P(), P(), P(None, every)),
        check_vma=False,
    )
```

```python
import math

import jax
import jax.numpy as jnp
from jax import lax
from jax.experimental import pallas as pl
from jax.experimental.pallas import tpu as pltpu
from jax.sharding import Mesh, PartitionSpec as P

HDIM = 128
BLK = 32
BLK_DEV = 4
NX, NY, NZ = 4, 8, 8
STRENGTH = 2.0
SCALING = HDIM**-0.5
MASKED = -1e30
BF = jnp.bfloat16
F32 = jnp.float32

PAIR = 4
REACH = 3


def dot(a, b, ca, cb):
    return lax.dot_general(a, b, (((ca,), (cb,)), ((), ())), preferred_element_type=F32)


def attention_kernel(
    q_ref, left_ref, own_ref, right_ref, fog_ref, low_ref, odp_ref, bias_ref,
    send_ref, to_left_ref, to_own_ref, to_right_ref, kv_ref, sum_ref, dq_ref, attn_ref,
):
    edge, tokens = left_ref.shape[0], own_ref.shape[0]
    rank = odp_ref.shape[1]
    kv_ref[:edge] = left_ref[...]
    kv_ref[edge : edge + tokens] = own_ref[...]
    kv_ref[edge + tokens :] = right_ref[...]
    sum_ref[...] = jnp.zeros_like(sum_ref)
    low_out = jnp.concatenate([low_ref[1][:, :rank], low_ref[3][:, :rank]], axis=0)
    dout = (fog_ref[...].astype(F32) + STRENGTH * dot(low_out, odp_ref[...], 1, 1)).astype(BF)
    block = tokens // 2
    wide = block + 2 * edge
    for j in range(2):
        rows = slice(j * block, (j + 1) * block)
        window = slice(j * block, j * block + wide)
        q, dout_j = q_ref[rows], dout[rows]
        k, v = kv_ref[window, :HDIM], kv_ref[window, HDIM:]
        s = (dot(q, k, 1, 1) * SCALING).reshape(8, BLK, wide)
        s = (s + bias_ref[8 * j : 8 * j + 8, window][:, None, :]).reshape(block, wide)
        weights = jnp.exp(s - s.max(axis=1, keepdims=True))
        probs = weights * (1.0 / weights.sum(axis=1, keepdims=True))
        probs_low = probs.astype(BF)
        attn = dot(probs_low, v, 1, 0).astype(BF)
        delta = (dout_j.astype(F32) * attn.astype(F32)).sum(axis=1, keepdims=True)
        dscore = (probs * (dot(dout_j, v, 1, 1) - delta)).astype(BF)
        attn_ref[rows] = attn
        dq_ref[rows] = (dot(dscore, k, 1, 0) * SCALING).astype(BF)
        sum_ref[window, :HDIM] += dot(dscore, q, 0, 0) * SCALING
        sum_ref[window, HDIM:] += dot(probs_low, dout_j, 0, 0)
    to_left_ref[...] = sum_ref[:edge].astype(BF)
    to_own_ref[...] = sum_ref[edge : edge + tokens]
    to_right_ref[...] = sum_ref[edge + tokens :].astype(BF)
    for yl in range(2):
        chip = slice(yl * block, (yl + 1) * block)
        later = slice(yl * block + block // 2, (yl + 1) * block)
        send_ref[2 * yl, :block] = dq_ref[chip]
        send_ref[2 * yl, block:] = dq_ref[later]
        send_ref[2 * yl + 1, :block] = attn_ref[chip]
        send_ref[2 * yl + 1, block:] = dq_ref[later]


def attention(q, left, own, right, fog, low, odp_head, bias):
    tokens, edge = q.shape[0], left.shape[0]
    shape = jax.ShapeDtypeStruct
    vmem = pl.BlockSpec(memory_space=pltpu.VMEM)
    return pl.pallas_call(
        attention_kernel,
        out_shape=[
            shape((PAIR, 3 * tokens // PAIR, HDIM), BF),
            shape((edge, 2 * HDIM), BF),
            shape((tokens, 2 * HDIM), F32),
            shape((edge, 2 * HDIM), BF),
        ],
        in_specs=[vmem] * 8,
        out_specs=[vmem] * 4,
        scratch_shapes=[
            pltpu.VMEM((tokens + 2 * edge, 2 * HDIM), BF),
            pltpu.VMEM((tokens + 2 * edge, 2 * HDIM), F32),
            pltpu.VMEM((tokens, HDIM), BF),
            pltpu.VMEM((tokens, HDIM), BF),
        ],
        compiler_params=pltpu.CompilerParams(vmem_limit_bytes=24 * 1024 * 1024),
        cost_estimate=pl.CostEstimate(flops=700_000_000, bytes_accessed=3_000_000, transcendentals=524288),
        name="attention",
    )(q, left, own, right, fog, low, odp_head, bias)


def merge_kernel(own_ref, from_left_ref, from_right_ref, send_ref, total_ref):
    tokens = own_ref.shape[0]
    frame = tokens // PAIR
    edge = from_left_ref.shape[0]
    head, tail = from_left_ref[...].astype(F32), from_right_ref[...].astype(F32)
    total_ref[:frame] = (own_ref[:frame] + head[:frame]).astype(BF)
    total_ref[frame:edge] = (own_ref[frame:edge] + head[frame:] + tail[: edge - frame]).astype(BF)
    total_ref[edge:] = (own_ref[edge:] + tail[edge - frame :]).astype(BF)
    for yl in range(2):
        chip = slice(2 * yl * frame, 2 * (yl + 1) * frame)
        for core in range(2):
            mine = slice((2 * yl + core) * frame, (2 * yl + core + 1) * frame)
            role = slice(core * HDIM, (core + 1) * HDIM)
            rest = slice((1 - core) * HDIM, (2 - core) * HDIM)
            send_ref[2 * yl + core, : 2 * frame] = total_ref[chip, role]
            send_ref[2 * yl + core, 2 * frame :] = total_ref[mine, rest]


def merge(own, from_left, from_right):
    tokens = own.shape[0]
    vmem = pl.BlockSpec(memory_space=pltpu.VMEM)
    return pl.pallas_call(
        merge_kernel,
        out_shape=jax.ShapeDtypeStruct((PAIR, 3 * tokens // PAIR, HDIM), BF),
        in_specs=[vmem] * 3,
        out_specs=vmem,
        scratch_shapes=[pltpu.VMEM((tokens, 2 * HDIM), BF)],
        compiler_params=pltpu.CompilerParams(vmem_limit_bytes=8 * 1024 * 1024),
        cost_estimate=pl.CostEstimate(flops=1_000_000, bytes_accessed=1_400_000, transcendentals=0),
        name="merge",
    )(own, from_left, from_right)


Z_STEP = 2


def low_kernel(core_ref, xo_ref, xt_ref, yo_ref, yt_ref, w_ref, low_ref, own_acc, other_acc):
    core = core_ref[0]
    step = pl.program_id(0)
    rows = xo_ref.shape[0]
    ranks = w_ref.shape[3]
    block = NX * w_ref.shape[2]

    @pl.when(step == 0)
    def _():
        own_acc[...] = jnp.zeros_like(own_acc)
        other_acc[...] = jnp.zeros_like(other_acc)

    lane = lax.broadcasted_iota(jnp.int32, (rows, ranks), 1)
    from_y = (lane < ranks // 2) & (core == 1)
    for zz in range(Z_STEP):
        cols = slice(zz * block, (zz + 1) * block)
        w = jnp.concatenate([w_ref[i, zz] for i in range(NX)], axis=0)
        for x_ref, y_ref, acc in ((xo_ref, yo_ref, own_acc), (xt_ref, yt_ref, other_acc)):
            acc[...] += jnp.where(from_y, dot(y_ref[:, cols], w, 1, 0), dot(x_ref[:, cols], w, 1, 0))

    @pl.when(step == pl.num_programs(0) - 1)
    def _():
        low_ref[pl.ds(pl.multiple_of(core * rows, rows), rows)] = own_acc[...].astype(BF)
        low_ref[pl.ds(pl.multiple_of((1 - core) * rows, rows), rows)] = other_acc[...].astype(BF)


def low_factors(core, x_own, x_other, y_own, y_other, weights):
    rows, width = x_own.shape
    pieces, ranks = weights.shape[2:]
    wide = pl.BlockSpec((rows, width * Z_STEP // NZ), lambda i: (0, i))
    return pl.pallas_call(
        low_kernel,
        grid=(NZ // Z_STEP,),
        out_shape=jax.ShapeDtypeStruct((2 * rows, ranks), BF),
        in_specs=[pl.BlockSpec(memory_space=pltpu.SMEM)] + [wide] * 4
        + [pl.BlockSpec((NX, Z_STEP, pieces, ranks), lambda i: (0, i, 0, 0))],
        out_specs=pl.BlockSpec((2 * rows, ranks), lambda i: (0, 0)),
        scratch_shapes=[pltpu.VMEM((rows, ranks), F32), pltpu.VMEM((rows, ranks), F32)],
        compiler_params=pltpu.CompilerParams(vmem_limit_bytes=10 * 1024 * 1024),
        cost_estimate=pl.CostEstimate(flops=700_000_000, bytes_accessed=6_600_000, transcendentals=0),
        name="low_factors",
    )(core, x_own, x_other, y_own, y_other, weights)


def grad_kernel(
    scale, core_ref, xo_ref, xt_ref, yo_ref, yt_ref, got_a_ref, got_b_ref, low_ref, m_a_ref, m_b_ref,
    g_ref, f_ref, u_ref,
):
    core = core_ref[0]
    step = pl.program_id(0)
    rows = xo_ref.shape[0]
    rank = m_a_ref.shape[1]
    block = xo_ref.shape[1] // Z_STEP
    piece = block // NX
    extra = g_ref.shape[2] - piece

    @pl.when(step == 0)
    def _():
        for i, (got_ref, m_ref) in enumerate(((got_a_ref, m_a_ref), (got_b_ref, m_b_ref))):
            ranks = slice(i * rank, (i + 1) * rank)
            low = low_ref[:, ranks]
            factor = None
            for head in range(PAIR):
                cols = slice(head * HDIM, (head + 1) * HDIM)
                got = got_ref[head, : 2 * rows]
                term = dot(got, m_ref[cols], 1, 0)
                factor = term if factor is None else factor + term
                u_ref[ranks, cols] = (dot(low, got, 0, 0) * scale).astype(BF)
            f_ref[:, ranks] = factor.astype(BF)

    f_own = f_ref[pl.ds(pl.multiple_of(core * rows, rows), rows)]
    f_other = f_ref[pl.ds(pl.multiple_of((1 - core) * rows, rows), rows)]
    line = lax.broadcasted_iota(jnp.int32, (2 * rank, block), 0)
    from_y = (line < rank) & (core == 1)
    for zz in range(Z_STEP):
        cols = slice(zz * block, (zz + 1) * block)
        gx = dot(f_own, xo_ref[:, cols], 0, 0) + dot(f_other, xt_ref[:, cols], 0, 0)
        gy = dot(f_own, yo_ref[:, cols], 0, 0) + dot(f_other, yt_ref[:, cols], 0, 0)
        g = (jnp.where(from_y, gy, gx) * scale).T.astype(BF)
        at = pl.ds(pl.multiple_of((step * Z_STEP + zz) * extra, extra), extra)
        for i in range(NX):
            g_ref[i, zz, :piece] = g[i * piece : (i + 1) * piece]
            g_ref[i, zz, piece:] = u_ref[at, i * 2 * rank : (i + 1) * 2 * rank]


def grad_partials(scale, core, x_own, x_other, y_own, y_other, got_a, got_b, low, m_a, m_b):
    rows, width = x_own.shape
    feats, rank = m_a.shape
    piece = width // (NX * NZ)
    extra = 2 * rank // NZ
    wide = pl.BlockSpec((rows, width * Z_STEP // NZ), lambda i: (0, i))
    whole = [pl.BlockSpec(a.shape, lambda i: (0, 0, 0)) for a in (got_a, got_b)]
    whole += [pl.BlockSpec(a.shape, lambda i: (0, 0)) for a in (low, m_a, m_b)]
    return pl.pallas_call(
        lambda *refs: grad_kernel(scale, *refs),
        grid=(NZ // Z_STEP,),
        out_shape=jax.ShapeDtypeStruct((NX, NZ, piece + extra, 2 * rank), BF),
        in_specs=[pl.BlockSpec(memory_space=pltpu.SMEM)] + [wide] * 4 + whole,
        out_specs=pl.BlockSpec((NX, Z_STEP, piece + extra, 2 * rank), lambda i: (0, i, 0, 0)),
        scratch_shapes=[pltpu.VMEM((2 * rows, 2 * rank), BF), pltpu.VMEM((2 * rank, feats), BF)],
        compiler_params=pltpu.CompilerParams(vmem_limit_bytes=16 * 1024 * 1024),
        cost_estimate=pl.CostEstimate(flops=800_000_000, bytes_accessed=7_500_000, transcendentals=0),
        name="grad_partials",
    )(core, x_own, x_other, y_own, y_other, got_a, got_b, low, m_a, m_b)


def exchange(parts, axes):
    return lax.all_to_all(parts, axes, split_axis=0, concat_axis=0, tiled=True)


def spread(block, axes, peers):
    return exchange(jnp.broadcast_to(block[None], (peers,) + block.shape), axes)


def across(block, by):
    return lax.ppermute(block, ("yl", "c"), [(i, i ^ by) for i in range(PAIR)])


def swap(block):
    return lax.ppermute(block, "c", [(0, 1), (1, 0)])


def pair_shift(block, by):
    pairs = NX * NY // 2
    return lax.ppermute(block, ("x", "yh"), [(i, i + by) for i in range(pairs) if 0 <= i + by < pairs])


def shards(
    inputs, queries, key_rows, values, frozen_output_gradient, out_grad, block_lists,
    down_qkv, up_qkv, output_down_projection, up_out,
):
    x_own, y_own = inputs[0], out_grad[0]
    rows, feats = queries.shape[1:]
    rank = output_down_projection.shape[1]
    own_cols = down_qkv.shape[1]
    slots = block_lists.shape[2]
    core = lax.axis_index("c")
    first = core == 0
    head = lax.axis_index(("yl", "c"))
    pair = lax.axis_index(("x", "yh"))
    line_axes = ("yh", "yl", "c")
    grad_scale = STRENGTH / math.sqrt(NX * NY * NZ * 2 * rows)
    core_id = core.astype(jnp.int32).reshape(1)

    stack = jnp.concatenate([queries[0], frozen_output_gradient[0], key_rows[0], values[0]], axis=0)
    lists = jnp.pad(block_lists[0].astype(BF), ((0, 12), (0, HDIM - slots)))
    shard = jnp.concatenate([down_qkv[0], down_qkv[1], up_out.T, down_qkv[2]], axis=1)
    copies = jnp.broadcast_to(shard.reshape(1, 2, -1), (2 * NY, 2, 2 * own_cols * rank))
    copies, stack = lax.optimization_barrier((copies, stack))
    line = exchange(copies, line_axes).reshape(2 * NY * own_cols, 4 * rank)
    line = lax.dynamic_slice_in_dim(line, core * 2 * rank, 2 * rank, 1)

    def for_head(h):
        return jnp.concatenate([lax.dynamic_slice_in_dim(stack, h * HDIM, HDIM, 1), lists], axis=0)

    got = [for_head(head)] + [across(for_head(head ^ by), by) for by in range(1, PAIR)]
    frames = [
        jnp.where(head == f, got[0], jnp.where(head ^ f == 1, got[1], jnp.where(head ^ f == 2, got[2], got[3])))
        for f in range(PAIR)
    ]
    frames = jnp.stack(frames)
    line, frames = lax.optimization_barrier((line, frames))
    q_pair, fog_pair, k_pair, v_pair = (
        frames[:, i * rows : (i + 1) * rows].reshape(PAIR * rows, HDIM) for i in range(4)
    )
    kv_pair = jnp.concatenate([k_pair, v_pair], axis=1)
    lists_pair = frames[:, 4 * rows : 4 * rows + BLK_DEV, :slots].reshape(PAIR * BLK_DEV, slots)
    left = pair_shift(kv_pair[rows:], 1)
    right = pair_shift(kv_pair[: REACH * rows], -1)
    window = (PAIR + 2 * REACH) * BLK_DEV
    ids = (PAIR * pair - REACH) * BLK_DEV + jnp.arange(window, dtype=jnp.int32)
    allowed = jnp.any(lists_pair[:, :, None] == ids.astype(F32)[None, None, :], axis=1) & (ids >= 0)[None]
    bias = jnp.repeat(jnp.where(allowed, 0.0, MASKED).astype(F32), BLK, axis=1)

    plane = spread(line, "z", NZ)
    plane, left, right, x_own, y_own = lax.optimization_barrier((plane, left, right, x_own, y_own))
    x_other = swap(x_own)
    y_other = lax.ppermute(y_own, "c", [(0, 1)])
    weights = spread(plane.reshape(-1, 2 * rank), "x", NX).reshape(NX, NZ, -1, 2 * rank)
    low = low_factors(core_id, x_own, x_other, y_own, y_other, weights)
    low_pair = lax.all_gather(low, ("yl", "c"))
    odp_head = lax.dynamic_slice_in_dim(output_down_projection, head * HDIM, HDIM, 0)

    send_a, to_left, to_own, to_right = attention(
        q_pair, left, kv_pair, right, fog_pair, low_pair, odp_head, bias
    )
    from_right = pair_shift(to_left, -1)
    from_left = pair_shift(to_right, 1)
    got_a = exchange(send_a, ("yl", "c"))
    m_a = jnp.where(first, up_qkv[0].T, output_down_projection)
    m_b = jnp.where(first, up_qkv[1].T, up_qkv[2].T)
    got_b = exchange(merge(to_own, from_left, from_right), ("yl", "c"))
    g = grad_partials(
        grad_scale, core_id, x_own, x_other, y_own, y_other, got_a, got_b, low, m_a, m_b
    )

    line_rows = 2 * NY * own_cols
    u_rows = g.shape[2] - line_rows
    step = exchange(g.reshape(NX, -1, 2 * rank), "x")
    step = step.astype(F32).sum(axis=0).astype(BF).reshape(NZ, -1, 2 * rank)
    step = exchange(step, "z")
    step = step.astype(F32).sum(axis=0).astype(BF)
    g_line = step[:line_rows].reshape(2 * NY, own_cols, 2 * rank)
    u_line = jnp.broadcast_to(step[line_rows:][None], (2 * NY, u_rows, 2 * rank))
    step = exchange(jnp.concatenate([g_line, u_line], axis=1), line_axes)
    step = step.reshape(NY, 2, own_cols + u_rows, 2 * rank).astype(F32).sum(axis=0)
    g_out = step[:, :own_cols]
    grad_down = jnp.stack([g_out[0, :, :rank], g_out[0, :, rank:], g_out[1, :, rank:]])
    grad_up_out = g_out[1, :, :rank].T
    u_mine = step[:, own_cols:].astype(BF).reshape(2 * u_rows, 2 * rank)
    u_all = spread(u_mine, ("x", "z"), NX * NZ).reshape(NX, NZ, 2, u_rows, 2 * rank)
    u_all = jnp.transpose(u_all, (2, 1, 3, 0, 4)).reshape(2, 2, rank, feats).astype(F32)
    grad_up = jnp.stack([u_all[0, 0], u_all[0, 1], u_all[1, 1]])
    grad_down_out = u_all[1, 0].T

    def own_frame(on_zero, on_one):
        return jnp.concatenate([jnp.where(first, on_zero[h], on_one[h]) for h in range(PAIR)], axis=1)[None]

    grad_q = own_frame(got_a[:, :rows], got_a[:, 2 * rows :])
    grad_k = own_frame(got_b[:, :rows], got_b[:, 2 * rows :])
    grad_v = own_frame(got_b[:, 2 * rows :], got_b[:, rows : 2 * rows])
    return grad_q, grad_k, grad_v, grad_down, grad_up, grad_down_out, grad_up_out


def solution(mesh):
    fine = Mesh(mesh.devices.reshape(NZ, NX, NY // 2, 2, 2), ("z", "x", "yh", "yl", "c"))
    ctx = ("x", "yh", "yl", "c")
    every = ("z",) + ctx
    tokens = P("z", ctx, None)
    return jax.shard_map(
        shards,
        mesh=fine,
        in_specs=(tokens,) * 7 + (P(None, every, None), P(), P(), P(None, every)),
        out_specs=(tokens,) * 3 + (P(None, every, None), P(), P(), P(None, every)),
        check_vma=False,
    )
```

```python
import math

import jax
import jax.numpy as jnp
from jax import lax
from jax.experimental import pallas as pl
from jax.experimental.pallas import tpu as pltpu
from jax.sharding import Mesh, PartitionSpec as P

HDIM = 128
BLK = 32
BLK_DEV = 4
NX, NY, NZ = 4, 8, 8
STRENGTH = 2.0
SCALING = HDIM**-0.5
MASKED = -1e30
BF = jnp.bfloat16
F32 = jnp.float32

SEGMENTS = ((0, 128), (128, 384), (384, 640), (640, 896), (896, 1024))


def dot(a, b, ca, cb):
    return lax.dot_general(a, b, (((ca,), (cb,)), ((), ())), preferred_element_type=F32)


def attention_kernel(
    core_ref, q_ref, l2_ref, l1_ref, own_ref, r1_ref, r2_ref, fog_ref, low_ref, odp_ref, bias_ref,
    kept_ref, send_ref, dq_ref, pl2_ref, pl1_ref, pown_ref, pr1_ref, pr2_ref, attn_ref, kv_ref,
):
    part_refs = (pl2_ref, pl1_ref, pown_ref, pr1_ref, pr2_ref)
    rows, half = q_ref.shape
    for ref, (a, b) in zip((l2_ref, l1_ref, own_ref, r1_ref, r2_ref), SEGMENTS):
        kv_ref[a:b] = ref[...]
    window = kv_ref.shape[0]
    dout = (fog_ref[...].astype(F32) + STRENGTH * dot(low_ref[1][:, : odp_ref.shape[1]], odp_ref[...], 1, 1)).astype(BF)
    bias = bias_ref[...]
    for head in range(half // HDIM):
        cols = slice(head * HDIM, (head + 1) * HDIM)
        vcols = slice(half + head * HDIM, half + (head + 1) * HDIM)
        q, dout_h = q_ref[:, cols], dout[:, cols]
        k, v = kv_ref[:, cols], kv_ref[:, vcols]
        s = (dot(q, k, 1, 1) * SCALING).reshape(8, BLK, window)
        s = (s + bias[:, None, :]).reshape(rows, window)
        weights = jnp.exp(s - s.max(axis=1, keepdims=True))
        probs = weights * (1.0 / weights.sum(axis=1, keepdims=True))
        probs_low = probs.astype(BF)
        attn = dot(probs_low, v, 1, 0).astype(BF)
        attn_ref[:, cols] = attn
        delta = (dout_h.astype(F32) * attn.astype(F32)).sum(axis=1, keepdims=True)
        dscore = (probs * (dot(dout_h, v, 1, 1) - delta)).astype(BF)
        dq_ref[:, cols] = (dot(dscore, k, 1, 0) * SCALING).astype(BF)
        dk = dot(dscore, q, 0, 0) * SCALING
        dv = dot(probs_low, dout_h, 0, 0)
        for ref, (a, b) in zip(part_refs, SEGMENTS):
            ref[:, cols] = dk[a:b].astype(ref.dtype)
            ref[:, vcols] = dv[a:b].astype(ref.dtype)

    @pl.when(core_ref[0] == 0)
    def _():
        kept_ref[...] = dq_ref[...]
        send_ref[:rows] = attn_ref[...]

    @pl.when(core_ref[0] != 0)
    def _():
        kept_ref[...] = attn_ref[...]
        send_ref[:rows] = dq_ref[...]

    send_ref[rows:] = dq_ref[rows // 2 :]


def attention(core, q, windows, fog, low, odp_half, bias):
    rows, half = q.shape
    shape = jax.ShapeDtypeStruct
    outs = [shape((rows, half), BF), shape((rows + rows // 2, half), BF), shape((rows, half), BF)]
    outs += [shape((b - a, 2 * half), F32 if i == 2 else BF) for i, (a, b) in enumerate(SEGMENTS)]
    vmem = pl.BlockSpec(memory_space=pltpu.VMEM)
    return pl.pallas_call(
        attention_kernel,
        out_shape=outs,
        in_specs=[pl.BlockSpec(memory_space=pltpu.SMEM)] + [vmem] * 10,
        out_specs=[vmem] * 8,
        scratch_shapes=[pltpu.VMEM((rows, half), BF), pltpu.VMEM((SEGMENTS[-1][1], 2 * half), BF)],
        compiler_params=pltpu.CompilerParams(vmem_limit_bytes=40 * 1024 * 1024),
        cost_estimate=pl.CostEstimate(flops=700_000_000, bytes_accessed=4_000_000, transcendentals=524288),
        name="attention",
    )(core, q, *windows, fog, low, odp_half, bias)


Z_STEP = 2


def low_kernel(core_ref, xo_ref, xt_ref, yo_ref, yt_ref, w_ref, low_ref, own_acc, other_acc):
    core = core_ref[0]
    step = pl.program_id(0)
    rows = xo_ref.shape[0]
    ranks = w_ref.shape[3]
    block = NX * w_ref.shape[2]

    @pl.when(step == 0)
    def _():
        own_acc[...] = jnp.zeros_like(own_acc)
        other_acc[...] = jnp.zeros_like(other_acc)

    lane = lax.broadcasted_iota(jnp.int32, (rows, ranks), 1)
    from_y = (lane < ranks // 2) & (core == 1)
    for zz in range(Z_STEP):
        cols = slice(zz * block, (zz + 1) * block)
        w = jnp.concatenate([w_ref[i, zz] for i in range(NX)], axis=0)
        for x_ref, y_ref, acc in ((xo_ref, yo_ref, own_acc), (xt_ref, yt_ref, other_acc)):
            acc[...] += jnp.where(from_y, dot(y_ref[:, cols], w, 1, 0), dot(x_ref[:, cols], w, 1, 0))

    @pl.when(step == pl.num_programs(0) - 1)
    def _():
        low_ref[pl.ds(pl.multiple_of(core * rows, rows), rows)] = own_acc[...].astype(BF)
        low_ref[pl.ds(pl.multiple_of((1 - core) * rows, rows), rows)] = other_acc[...].astype(BF)


def low_factors(core, x_own, x_other, y_own, y_other, weights):
    rows, width = x_own.shape
    pieces, ranks = weights.shape[2:]
    wide = pl.BlockSpec((rows, width * Z_STEP // NZ), lambda i: (0, i))
    return pl.pallas_call(
        low_kernel,
        grid=(NZ // Z_STEP,),
        out_shape=jax.ShapeDtypeStruct((2 * rows, ranks), BF),
        in_specs=[pl.BlockSpec(memory_space=pltpu.SMEM)] + [wide] * 4
        + [pl.BlockSpec((NX, Z_STEP, pieces, ranks), lambda i: (0, i, 0, 0))],
        out_specs=pl.BlockSpec((2 * rows, ranks), lambda i: (0, 0)),
        scratch_shapes=[pltpu.VMEM((rows, ranks), F32), pltpu.VMEM((rows, ranks), F32)],
        compiler_params=pltpu.CompilerParams(vmem_limit_bytes=24 * 1024 * 1024),
        cost_estimate=pl.CostEstimate(flops=700_000_000, bytes_accessed=6_600_000, transcendentals=0),
        name="low_factors",
    )(core, x_own, x_other, y_own, y_other, weights)


def grad_kernel(
    scale, core_ref, xo_ref, xt_ref, yo_ref, yt_ref, kept_a_ref, got_a_ref, kept_b_ref, got_b_ref, low_ref,
    m_a_ref, m_b_ref, g_ref, f_ref, u_ref,
):
    core = core_ref[0]
    step = pl.program_id(0)
    rows = xo_ref.shape[0]
    half = kept_a_ref.shape[1]
    rank = m_a_ref.shape[1]
    block = xo_ref.shape[1] // Z_STEP
    piece = block // NX
    extra = g_ref.shape[2] - piece
    mine = pl.ds(pl.multiple_of(core * half, half), half)
    theirs = pl.ds(pl.multiple_of((1 - core) * half, half), half)

    @pl.when(step == 0)
    def _():
        for i, (kept_ref, got_ref, m_ref) in enumerate(
            ((kept_a_ref, got_a_ref, m_a_ref), (kept_b_ref, got_b_ref, m_b_ref))
        ):
            kept, got = kept_ref[...], got_ref[: 2 * rows]
            ranks = slice(i * rank, (i + 1) * rank)
            low = low_ref[:, ranks]
            f_ref[:, ranks] = (dot(kept, m_ref[mine], 1, 0) + dot(got, m_ref[theirs], 1, 0)).astype(BF)
            u_ref[ranks, mine] = (dot(low, kept, 0, 0) * scale).astype(BF)
            u_ref[ranks, theirs] = (dot(low, got, 0, 0) * scale).astype(BF)

    f_own = f_ref[pl.ds(pl.multiple_of(core * rows, rows), rows)]
    f_other = f_ref[pl.ds(pl.multiple_of((1 - core) * rows, rows), rows)]
    line = lax.broadcasted_iota(jnp.int32, (2 * rank, block), 0)
    from_y = (line < rank) & (core == 1)
    for zz in range(Z_STEP):
        cols = slice(zz * block, (zz + 1) * block)
        gx = dot(f_own, xo_ref[:, cols], 0, 0) + dot(f_other, xt_ref[:, cols], 0, 0)
        gy = dot(f_own, yo_ref[:, cols], 0, 0) + dot(f_other, yt_ref[:, cols], 0, 0)
        g = (jnp.where(from_y, gy, gx) * scale).T.astype(BF)
        at = pl.ds(pl.multiple_of((step * Z_STEP + zz) * extra, extra), extra)
        for i in range(NX):
            g_ref[i, zz, :piece] = g[i * piece : (i + 1) * piece]
            g_ref[i, zz, piece:] = u_ref[at, i * 2 * rank : (i + 1) * 2 * rank]


def grad_partials(scale, core, x_own, x_other, y_own, y_other, kept_a, got_a, kept_b, got_b, low, m_a, m_b):
    rows, width = x_own.shape
    feats, rank = m_a.shape
    piece = width // (NX * NZ)
    extra = 2 * rank // NZ
    wide = pl.BlockSpec((rows, width * Z_STEP // NZ), lambda i: (0, i))
    whole = [pl.BlockSpec(a.shape, lambda i: (0, 0)) for a in (kept_a, got_a, kept_b, got_b, low, m_a, m_b)]
    return pl.pallas_call(
        lambda *refs: grad_kernel(scale, *refs),
        grid=(NZ // Z_STEP,),
        out_shape=jax.ShapeDtypeStruct((NX, NZ, piece + extra, 2 * rank), BF),
        in_specs=[pl.BlockSpec(memory_space=pltpu.SMEM)] + [wide] * 4 + whole,
        out_specs=pl.BlockSpec((NX, Z_STEP, piece + extra, 2 * rank), lambda i: (0, i, 0, 0)),
        scratch_shapes=[pltpu.VMEM((2 * rows, 2 * rank), BF), pltpu.VMEM((2 * rank, feats), BF)],
        compiler_params=pltpu.CompilerParams(vmem_limit_bytes=24 * 1024 * 1024),
        cost_estimate=pl.CostEstimate(flops=800_000_000, bytes_accessed=7_500_000, transcendentals=0),
        name="grad_partials",
    )(core, x_own, x_other, y_own, y_other, kept_a, got_a, kept_b, got_b, low, m_a, m_b)


def exchange(parts, axes):
    return lax.all_to_all(parts, axes, split_axis=0, concat_axis=0, tiled=True)


def spread(block, axes, peers):
    return exchange(jnp.broadcast_to(block[None], (peers,) + block.shape), axes)


def swap(block):
    return lax.ppermute(block, "c", [(0, 1), (1, 0)])


def chip_shift(block, by):
    chips = NX * NY
    return lax.ppermute(block, ("x", "y"), [(i, i + by) for i in range(chips) if 0 <= i + by < chips])


def shards(
    inputs, queries, key_rows, values, frozen_output_gradient, out_grad, block_lists,
    down_qkv, up_qkv, output_down_projection, up_out,
):
    x_own, y_own = inputs[0], out_grad[0]
    rows, feats = queries.shape[1:]
    half = feats // 2
    rank = output_down_projection.shape[1]
    width = x_own.shape[1]
    own_cols = down_qkv.shape[1]
    core = lax.axis_index("c")
    first = core == 0
    chip = lax.axis_index("x") * NY + lax.axis_index("y")
    grad_scale = STRENGTH / math.sqrt(NX * NY * NZ * 2 * rows)

    core_id = core.astype(jnp.int32).reshape(1)

    stack = jnp.concatenate([queries[0], frozen_output_gradient[0], key_rows[0], values[0]], axis=0)

    shard = jnp.concatenate([down_qkv[0], down_qkv[1], up_out.T, down_qkv[2]], axis=1)
    copies = jnp.broadcast_to(shard.reshape(1, 2, -1), (2 * NY, 2, 2 * own_cols * rank))
    copies, stack = lax.optimization_barrier((copies, stack))
    line = exchange(copies, ("y", "c")).reshape(2 * NY * own_cols, 4 * rank)
    line = lax.dynamic_slice_in_dim(line, core * 2 * rank, 2 * rank, 1)

    lists = jnp.pad(block_lists[0].astype(BF), ((0, 12), (0, half - block_lists.shape[2])))
    kept = jnp.concatenate([jnp.where(first, stack[:, :half], stack[:, half:]), lists], axis=0)
    got = swap(jnp.concatenate([jnp.where(first, stack[:, half:], stack[:, :half]), lists], axis=0))
    chip_stack = jnp.stack([jnp.where(first, kept, got), jnp.where(first, got, kept)])
    x_other = swap(x_own)
    y_other = lax.ppermute(y_own, "c", [(0, 1)])
    line, chip_stack = lax.optimization_barrier((line, chip_stack))

    q_chip = chip_stack[:, :rows].reshape(2 * rows, half)
    fog_chip = chip_stack[:, rows : 2 * rows].reshape(2 * rows, half)
    kv_chip = jnp.concatenate(
        [chip_stack[:, 2 * rows : 3 * rows], chip_stack[:, 3 * rows : 4 * rows]], axis=2
    ).reshape(2 * rows, 2 * half)
    lists_chip = chip_stack[:, 4 * rows : 4 * rows + BLK_DEV, : block_lists.shape[2]].reshape(
        2 * BLK_DEV, -1
    )
    l1, r1 = chip_shift(kv_chip, 1), chip_shift(kv_chip, -1)
    ids = (2 * chip - 3) * BLK_DEV + jnp.arange(8 * BLK_DEV, dtype=jnp.int32)
    allowed = jnp.any(lists_chip[:, :, None] == ids.astype(F32)[None, None, :], axis=1) & (ids >= 0)[None]
    bias = jnp.repeat(jnp.where(allowed, 0.0, MASKED).astype(F32), BLK, axis=1)

    plane = spread(line, "z", NZ)
    copies = jnp.broadcast_to(plane.reshape(1, -1, 2 * rank), (NX, NZ * plane.shape[1], 2 * rank))
    copies, l1, r1, kv_late = lax.optimization_barrier((copies, l1, r1, kv_chip))
    windows = (chip_shift(kv_late[rows:], 2), l1, kv_chip, r1, chip_shift(kv_late[:rows], -2))
    weights = exchange(copies, "x").reshape(NX, NZ, -1, 2 * rank)
    low = low_factors(core_id, x_own, x_other, y_own, y_other, weights)
    low_both = lax.all_gather(low, "c")
    odp_half = lax.dynamic_slice_in_dim(output_down_projection, core * half, half, 0)

    kept_a, send_a, dq, p_l2, p_l1, p_own, p_r1, p_r2 = attention(
        core_id, q_chip, windows, fog_chip, low_both, odp_half, bias
    )
    from_r1 = chip_shift(p_l1, -1)
    from_l1 = chip_shift(p_r1, 1)
    from_r2 = chip_shift(p_l2, -2)
    from_l2 = chip_shift(p_r2, 2)
    got_a = swap(send_a)
    m_a = jnp.where(first, up_qkv[0].T, output_down_projection)
    m_b = jnp.where(first, up_qkv[1].T, up_qkv[2].T)

    total = p_own + from_r1.astype(F32) + from_l1.astype(F32)
    total = total + jnp.concatenate([from_l2, from_r2], axis=0).astype(F32)
    total = total.astype(BF)
    dk, dv = total[:, :half], total[:, half:]
    kept_b = jnp.where(first, dk, dv)
    got_b = swap(
        jnp.concatenate([jnp.where(first, dv, dk), jnp.where(first, dk[rows:], dv[:rows])], axis=0)
    )
    g = grad_partials(
        grad_scale, core_id, x_own, x_other, y_own, y_other, kept_a, got_a, kept_b, got_b, low, m_a, m_b
    )

    line_rows = 2 * NY * own_cols
    u_rows = g.shape[2] - line_rows
    step = exchange(g.reshape(NX, -1, 2 * rank), "x")
    step = step.astype(F32).sum(axis=0).astype(BF).reshape(NZ, -1, 2 * rank)
    step = exchange(step, "z")
    step = step.astype(F32).sum(axis=0).astype(BF)
    g_line = step[:line_rows].reshape(2 * NY, own_cols, 2 * rank)
    u_line = jnp.broadcast_to(step[line_rows:][None], (2 * NY, u_rows, 2 * rank))
    step = exchange(jnp.concatenate([g_line, u_line], axis=1), ("y", "c"))
    step = step.reshape(NY, 2, own_cols + u_rows, 2 * rank).astype(F32).sum(axis=0)
    g_out = step[:, :own_cols]
    grad_down = jnp.stack([g_out[0, :, :rank], g_out[0, :, rank:], g_out[1, :, rank:]])
    grad_up_out = g_out[1, :, :rank].T
    u_mine = step[:, own_cols:].astype(BF).reshape(2 * u_rows, 2 * rank)
    u_all = spread(u_mine, ("x", "z"), NX * NZ).reshape(NX, NZ, 2, u_rows, 2 * rank)
    u_all = jnp.transpose(u_all, (2, 1, 3, 0, 4)).reshape(2, 2, rank, feats).astype(F32)
    grad_up = jnp.stack([u_all[0, 0], u_all[0, 1], u_all[1, 1]])
    grad_down_out = u_all[1, 0].T

    def own_frame(mine, from_zero, from_one):
        left = jnp.where(first, mine[:rows], from_zero)
        right = jnp.where(first, from_one, mine[rows:])
        return jnp.concatenate([left, right], axis=1)[None]

    grad_q = own_frame(dq, got_a[2 * rows :], got_a[:rows])
    grad_k = own_frame(dk, got_b[2 * rows :], got_b[:rows])
    grad_v = own_frame(dv, got_b[rows : 2 * rows], got_b[2 * rows :])
    return grad_q, grad_k, grad_v, grad_down, grad_up, grad_down_out, grad_up_out


def solution(mesh):
    fine = Mesh(mesh.devices.reshape(NZ, NX, NY, 2), ("z", "x", "y", "c"))
    ctx = ("x", "y", "c")
    every = ("z", "x", "y", "c")
    tokens = P("z", ctx, None)
    return jax.shard_map(
        shards,
        mesh=fine,
        in_specs=(tokens,) * 7 + (P(None, every, None), P(), P(), P(None, every)),
        out_specs=(tokens,) * 3 + (P(None, every, None), P(), P(), P(None, every)),
        check_vma=False,
    )
```

```python
import math

import jax
import jax.numpy as jnp
from jax import lax
from jax.experimental import pallas as pl
from jax.experimental.pallas import tpu as pltpu
from jax.sharding import Mesh, PartitionSpec as P

HDIM = 128
BLK = 32
BLK_DEV = 4
NX, NY, NZ = 4, 8, 8
STRENGTH = 2.0
SCALING = HDIM**-0.5
MASKED = -1e30
BF = jnp.bfloat16
F32 = jnp.float32

SEGMENTS = ((0, 128), (128, 384), (384, 640), (640, 896), (896, 1024))


def dot(a, b, ca, cb):
    return lax.dot_general(a, b, (((ca,), (cb,)), ((), ())), preferred_element_type=F32)


def attention_kernel(
    core_ref, q_ref, l2_ref, l1_ref, own_ref, r1_ref, r2_ref, fog_ref, low_ref, odp_ref, bias_ref,
    kept_ref, send_ref, dq_ref, pl2_ref, pl1_ref, pown_ref, pr1_ref, pr2_ref, attn_ref, kv_ref,
):
    part_refs = (pl2_ref, pl1_ref, pown_ref, pr1_ref, pr2_ref)
    rows, half = q_ref.shape
    for ref, (a, b) in zip((l2_ref, l1_ref, own_ref, r1_ref, r2_ref), SEGMENTS):
        kv_ref[a:b] = ref[...]
    window = kv_ref.shape[0]
    dout = (fog_ref[...].astype(F32) + STRENGTH * dot(low_ref[1][:, : odp_ref.shape[1]], odp_ref[...], 1, 1)).astype(BF)
    bias = bias_ref[...]
    for head in range(half // HDIM):
        cols = slice(head * HDIM, (head + 1) * HDIM)
        vcols = slice(half + head * HDIM, half + (head + 1) * HDIM)
        q, dout_h = q_ref[:, cols], dout[:, cols]
        k, v = kv_ref[:, cols], kv_ref[:, vcols]
        s = (dot(q, k, 1, 1) * SCALING).reshape(8, BLK, window)
        s = (s + bias[:, None, :]).reshape(rows, window)
        weights = jnp.exp(s - s.max(axis=1, keepdims=True))
        probs = weights * (1.0 / weights.sum(axis=1, keepdims=True))
        probs_low = probs.astype(BF)
        attn = dot(probs_low, v, 1, 0).astype(BF)
        attn_ref[:, cols] = attn
        delta = (dout_h.astype(F32) * attn.astype(F32)).sum(axis=1, keepdims=True)
        dscore = (probs * (dot(dout_h, v, 1, 1) - delta)).astype(BF)
        dq_ref[:, cols] = (dot(dscore, k, 1, 0) * SCALING).astype(BF)
        dk = dot(dscore, q, 0, 0) * SCALING
        dv = dot(probs_low, dout_h, 0, 0)
        for ref, (a, b) in zip(part_refs, SEGMENTS):
            ref[:, cols] = dk[a:b].astype(ref.dtype)
            ref[:, vcols] = dv[a:b].astype(ref.dtype)

    @pl.when(core_ref[0] == 0)
    def _():
        kept_ref[...] = dq_ref[...]
        send_ref[:rows] = attn_ref[...]

    @pl.when(core_ref[0] != 0)
    def _():
        kept_ref[...] = attn_ref[...]
        send_ref[:rows] = dq_ref[...]

    send_ref[rows:] = dq_ref[rows // 2 :]


def attention(core, q, windows, fog, low, odp_half, bias):
    rows, half = q.shape
    shape = jax.ShapeDtypeStruct
    outs = [shape((rows, half), BF), shape((rows + rows // 2, half), BF), shape((rows, half), BF)]
    outs += [shape((b - a, 2 * half), F32 if i == 2 else BF) for i, (a, b) in enumerate(SEGMENTS)]
    vmem = pl.BlockSpec(memory_space=pltpu.VMEM)
    return pl.pallas_call(
        attention_kernel,
        out_shape=outs,
        in_specs=[pl.BlockSpec(memory_space=pltpu.SMEM)] + [vmem] * 10,
        out_specs=[vmem] * 8,
        scratch_shapes=[pltpu.VMEM((rows, half), BF), pltpu.VMEM((SEGMENTS[-1][1], 2 * half), BF)],
        compiler_params=pltpu.CompilerParams(vmem_limit_bytes=40 * 1024 * 1024),
        cost_estimate=pl.CostEstimate(flops=700_000_000, bytes_accessed=4_000_000, transcendentals=524288),
        name="attention",
    )(core, q, *windows, fog, low, odp_half, bias)


Z_STEP = 2


def low_kernel(core_ref, xo_ref, xt_ref, yo_ref, yt_ref, w_ref, low_ref, own_acc, other_acc):
    core = core_ref[0]
    step = pl.program_id(0)
    rows = xo_ref.shape[0]
    ranks = w_ref.shape[3]
    block = NX * w_ref.shape[2]

    @pl.when(step == 0)
    def _():
        own_acc[...] = jnp.zeros_like(own_acc)
        other_acc[...] = jnp.zeros_like(other_acc)

    lane = lax.broadcasted_iota(jnp.int32, (rows, ranks), 1)
    from_y = (lane < ranks // 2) & (core == 1)
    for zz in range(Z_STEP):
        cols = slice(zz * block, (zz + 1) * block)
        w = jnp.concatenate([w_ref[i, zz] for i in range(NX)], axis=0)
        for x_ref, y_ref, acc in ((xo_ref, yo_ref, own_acc), (xt_ref, yt_ref, other_acc)):
            acc[...] += jnp.where(from_y, dot(y_ref[:, cols], w, 1, 0), dot(x_ref[:, cols], w, 1, 0))

    @pl.when(step == pl.num_programs(0) - 1)
    def _():
        low_ref[pl.ds(pl.multiple_of(core * rows, rows), rows)] = own_acc[...].astype(BF)
        low_ref[pl.ds(pl.multiple_of((1 - core) * rows, rows), rows)] = other_acc[...].astype(BF)


def low_factors(core, x_own, x_other, y_own, y_other, weights):
    rows, width = x_own.shape
    pieces, ranks = weights.shape[2:]
    wide = pl.BlockSpec((rows, width * Z_STEP // NZ), lambda i: (0, i))
    return pl.pallas_call(
        low_kernel,
        grid=(NZ // Z_STEP,),
        out_shape=jax.ShapeDtypeStruct((2 * rows, ranks), BF),
        in_specs=[pl.BlockSpec(memory_space=pltpu.SMEM)] + [wide] * 4
        + [pl.BlockSpec((NX, Z_STEP, pieces, ranks), lambda i: (0, i, 0, 0))],
        out_specs=pl.BlockSpec((2 * rows, ranks), lambda i: (0, 0)),
        scratch_shapes=[pltpu.VMEM((rows, ranks), F32), pltpu.VMEM((rows, ranks), F32)],
        compiler_params=pltpu.CompilerParams(vmem_limit_bytes=24 * 1024 * 1024),
        cost_estimate=pl.CostEstimate(flops=700_000_000, bytes_accessed=6_600_000, transcendentals=0),
        name="low_factors",
    )(core, x_own, x_other, y_own, y_other, weights)


def grad_kernel(
    scale, core_ref, xo_ref, xt_ref, yo_ref, yt_ref, kept_a_ref, got_a_ref, kept_b_ref, got_b_ref, low_ref,
    m_a_ref, m_b_ref, g_ref, f_ref, u_ref,
):
    core = core_ref[0]
    step = pl.program_id(0)
    rows = xo_ref.shape[0]
    half = kept_a_ref.shape[1]
    rank = m_a_ref.shape[1]
    block = xo_ref.shape[1] // Z_STEP
    piece = block // NX
    extra = g_ref.shape[2] - piece
    mine = pl.ds(pl.multiple_of(core * half, half), half)
    theirs = pl.ds(pl.multiple_of((1 - core) * half, half), half)

    @pl.when(step == 0)
    def _():
        for i, (kept_ref, got_ref, m_ref) in enumerate(
            ((kept_a_ref, got_a_ref, m_a_ref), (kept_b_ref, got_b_ref, m_b_ref))
        ):
            kept, got = kept_ref[...], got_ref[: 2 * rows]
            ranks = slice(i * rank, (i + 1) * rank)
            low = low_ref[:, ranks]
            f_ref[:, ranks] = (dot(kept, m_ref[mine], 1, 0) + dot(got, m_ref[theirs], 1, 0)).astype(BF)
            u_ref[ranks, mine] = (dot(low, kept, 0, 0) * scale).astype(BF)
            u_ref[ranks, theirs] = (dot(low, got, 0, 0) * scale).astype(BF)

    f_own = f_ref[pl.ds(pl.multiple_of(core * rows, rows), rows)]
    f_other = f_ref[pl.ds(pl.multiple_of((1 - core) * rows, rows), rows)]
    line = lax.broadcasted_iota(jnp.int32, (2 * rank, block), 0)
    from_y = (line < rank) & (core == 1)
    for zz in range(Z_STEP):
        cols = slice(zz * block, (zz + 1) * block)
        gx = dot(f_own, xo_ref[:, cols], 0, 0) + dot(f_other, xt_ref[:, cols], 0, 0)
        gy = dot(f_own, yo_ref[:, cols], 0, 0) + dot(f_other, yt_ref[:, cols], 0, 0)
        g = (jnp.where(from_y, gy, gx) * scale).T.astype(BF)
        at = pl.ds(pl.multiple_of((step * Z_STEP + zz) * extra, extra), extra)
        for i in range(NX):
            g_ref[i, zz, :piece] = g[i * piece : (i + 1) * piece]
            g_ref[i, zz, piece:] = u_ref[at, i * 2 * rank : (i + 1) * 2 * rank]


def grad_partials(scale, core, x_own, x_other, y_own, y_other, kept_a, got_a, kept_b, got_b, low, m_a, m_b):
    rows, width = x_own.shape
    feats, rank = m_a.shape
    piece = width // (NX * NZ)
    extra = 2 * rank // NZ
    wide = pl.BlockSpec((rows, width * Z_STEP // NZ), lambda i: (0, i))
    whole = [pl.BlockSpec(a.shape, lambda i: (0, 0)) for a in (kept_a, got_a, kept_b, got_b, low, m_a, m_b)]
    return pl.pallas_call(
        lambda *refs: grad_kernel(scale, *refs),
        grid=(NZ // Z_STEP,),
        out_shape=jax.ShapeDtypeStruct((NX, NZ, piece + extra, 2 * rank), BF),
        in_specs=[pl.BlockSpec(memory_space=pltpu.SMEM)] + [wide] * 4 + whole,
        out_specs=pl.BlockSpec((NX, Z_STEP, piece + extra, 2 * rank), lambda i: (0, i, 0, 0)),
        scratch_shapes=[pltpu.VMEM((2 * rows, 2 * rank), BF), pltpu.VMEM((2 * rank, feats), BF)],
        compiler_params=pltpu.CompilerParams(vmem_limit_bytes=24 * 1024 * 1024),
        cost_estimate=pl.CostEstimate(flops=800_000_000, bytes_accessed=7_500_000, transcendentals=0),
        name="grad_partials",
    )(core, x_own, x_other, y_own, y_other, kept_a, got_a, kept_b, got_b, low, m_a, m_b)


def exchange(parts, axes):
    return lax.all_to_all(parts, axes, split_axis=0, concat_axis=0, tiled=True)


def spread(block, axes, peers):
    return exchange(jnp.broadcast_to(block[None], (peers,) + block.shape), axes)


def swap(block):
    return lax.ppermute(block, "c", [(0, 1), (1, 0)])


def chip_shift(block, by):
    chips = NX * NY
    return lax.ppermute(block, ("x", "y"), [(i, i + by) for i in range(chips) if 0 <= i + by < chips])


def shards(
    inputs, queries, key_rows, values, frozen_output_gradient, out_grad, block_lists,
    down_qkv, up_qkv, output_down_projection, up_out,
):
    x_own, y_own = inputs[0], out_grad[0]
    rows, feats = queries.shape[1:]
    half = feats // 2
    rank = output_down_projection.shape[1]
    width = x_own.shape[1]
    own_cols = down_qkv.shape[1]
    core = lax.axis_index("c")
    first = core == 0
    chip = lax.axis_index("x") * NY + lax.axis_index("y")
    grad_scale = STRENGTH / math.sqrt(NX * NY * NZ * 2 * rows)

    core_id = core.astype(jnp.int32).reshape(1)

    shard = jnp.concatenate([down_qkv[0], down_qkv[1], up_out.T, down_qkv[2]], axis=1)
    copies = jnp.broadcast_to(shard.reshape(1, 2, -1), (2 * NY, 2, 2 * own_cols * rank))
    saved = (queries[0], frozen_output_gradient[0], key_rows[0], values[0])
    copies, saved = lax.optimization_barrier((copies, saved))
    stack = jnp.concatenate(saved, axis=0)
    line = exchange(copies, ("y", "c")).reshape(2 * NY * own_cols, 4 * rank)
    line = lax.dynamic_slice_in_dim(line, core * 2 * rank, 2 * rank, 1)

    lists = jnp.pad(block_lists[0].astype(BF), ((0, 12), (0, half - block_lists.shape[2])))
    kept = jnp.concatenate([jnp.where(first, stack[:, :half], stack[:, half:]), lists], axis=0)
    got = swap(jnp.concatenate([jnp.where(first, stack[:, half:], stack[:, :half]), lists], axis=0))
    chip_stack = jnp.stack([jnp.where(first, kept, got), jnp.where(first, got, kept)])
    x_other = swap(x_own)
    y_other = lax.ppermute(y_own, "c", [(0, 1)])
    line, chip_stack = lax.optimization_barrier((line, chip_stack))

    q_chip = chip_stack[:, :rows].reshape(2 * rows, half)
    fog_chip = chip_stack[:, rows : 2 * rows].reshape(2 * rows, half)
    kv_chip = jnp.concatenate(
        [chip_stack[:, 2 * rows : 3 * rows], chip_stack[:, 3 * rows : 4 * rows]], axis=2
    ).reshape(2 * rows, 2 * half)
    lists_chip = chip_stack[:, 4 * rows : 4 * rows + BLK_DEV, : block_lists.shape[2]].reshape(
        2 * BLK_DEV, -1
    )
    l1, r1 = chip_shift(kv_chip, 1), chip_shift(kv_chip, -1)
    ids = (2 * chip - 3) * BLK_DEV + jnp.arange(8 * BLK_DEV, dtype=jnp.int32)
    allowed = jnp.any(lists_chip[:, :, None] == ids.astype(F32)[None, None, :], axis=1) & (ids >= 0)[None]
    bias = jnp.repeat(jnp.where(allowed, 0.0, MASKED).astype(F32), BLK, axis=1)

    plane = spread(line, "z", NZ)
    copies = jnp.broadcast_to(plane.reshape(1, -1, 2 * rank), (NX, NZ * plane.shape[1], 2 * rank))
    copies, kv_late = lax.optimization_barrier((copies, kv_chip))
    windows = (chip_shift(kv_late[rows:], 2), l1, kv_chip, r1, chip_shift(kv_late[:rows], -2))
    weights = exchange(copies, "x").reshape(NX, NZ, -1, 2 * rank)
    low = low_factors(core_id, x_own, x_other, y_own, y_other, weights)
    m_a = jnp.where(first, up_qkv[0].T, output_down_projection)
    m_b = jnp.where(first, up_qkv[1].T, up_qkv[2].T)
    low, m_a, m_b = lax.optimization_barrier((low, m_a, m_b))
    low_both = lax.all_gather(low, "c")
    odp_half = lax.dynamic_slice_in_dim(output_down_projection, core * half, half, 0)

    kept_a, send_a, dq, p_l2, p_l1, p_own, p_r1, p_r2 = attention(
        core_id, q_chip, windows, fog_chip, low_both, odp_half, bias
    )
    from_r1 = chip_shift(p_l1, -1)
    from_l1 = chip_shift(p_r1, 1)
    from_r2 = chip_shift(p_l2, -2)
    from_l2 = chip_shift(p_r2, 2)
    got_a = swap(send_a)

    total = p_own + from_r1.astype(F32) + from_l1.astype(F32)
    total = total + jnp.concatenate([from_l2, from_r2], axis=0).astype(F32)
    total = total.astype(BF)
    dk, dv = total[:, :half], total[:, half:]
    kept_b = jnp.where(first, dk, dv)
    got_b = swap(
        jnp.concatenate([jnp.where(first, dv, dk), jnp.where(first, dk[rows:], dv[:rows])], axis=0)
    )
    g = grad_partials(
        grad_scale, core_id, x_own, x_other, y_own, y_other, kept_a, got_a, kept_b, got_b, low, m_a, m_b
    )

    line_rows = 2 * NY * own_cols
    u_rows = g.shape[2] - line_rows
    step = exchange(g.reshape(NX, -1, 2 * rank), "x")
    step = step.astype(F32).sum(axis=0).astype(BF).reshape(NZ, -1, 2 * rank)
    step = exchange(step, "z")
    step = step.astype(F32).sum(axis=0).astype(BF)
    g_line = step[:line_rows].reshape(2 * NY, own_cols, 2 * rank)
    u_line = jnp.broadcast_to(step[line_rows:][None], (2 * NY, u_rows, 2 * rank))
    step = exchange(jnp.concatenate([g_line, u_line], axis=1), ("y", "c"))
    step = step.reshape(NY, 2, own_cols + u_rows, 2 * rank).astype(F32).sum(axis=0)
    g_out = step[:, :own_cols]
    grad_down = jnp.stack([g_out[0, :, :rank], g_out[0, :, rank:], g_out[1, :, rank:]])
    grad_up_out = g_out[1, :, :rank].T
    u_mine = step[:, own_cols:].astype(BF).reshape(2 * u_rows, 2 * rank)
    u_all = spread(u_mine, ("x", "z"), NX * NZ).reshape(NX, NZ, 2, u_rows, 2 * rank)
    u_all = jnp.transpose(u_all, (2, 1, 3, 0, 4)).reshape(2, 2, rank, feats).astype(F32)
    grad_up = jnp.stack([u_all[0, 0], u_all[0, 1], u_all[1, 1]])
    grad_down_out = u_all[1, 0].T

    def own_frame(mine, from_zero, from_one):
        left = jnp.where(first, mine[:rows], from_zero)
        right = jnp.where(first, from_one, mine[rows:])
        return jnp.concatenate([left, right], axis=1)[None]

    grad_q = own_frame(dq, got_a[2 * rows :], got_a[:rows])
    grad_k = own_frame(dk, got_b[2 * rows :], got_b[:rows])
    grad_v = own_frame(dv, got_b[rows : 2 * rows], got_b[2 * rows :])
    return grad_q, grad_k, grad_v, grad_down, grad_up, grad_down_out, grad_up_out


def solution(mesh):
    fine = Mesh(mesh.devices.reshape(NZ, NX, NY, 2), ("z", "x", "y", "c"))
    ctx = ("x", "y", "c")
    every = ("z", "x", "y", "c")
    tokens = P("z", ctx, None)
    return jax.shard_map(
        shards,
        mesh=fine,
        in_specs=(tokens,) * 7 + (P(None, every, None), P(), P(), P(None, every)),
        out_specs=(tokens,) * 3 + (P(None, every, None), P(), P(), P(None, every)),
        check_vma=False,
    )
```

```python
import math

import jax
import jax.numpy as jnp
from jax import lax
from jax.experimental import pallas as pl
from jax.experimental.pallas import tpu as pltpu
from jax.sharding import Mesh, PartitionSpec as P

HDIM = 128
BLK = 32
BLK_DEV = 4
NX, NY, NZ = 4, 8, 8
STRENGTH = 2.0
SCALING = HDIM**-0.5
MASKED = -1e30
BF = jnp.bfloat16
F32 = jnp.float32

SEGMENTS = ((0, 128), (128, 384), (384, 640), (640, 896), (896, 1024))


def dot(a, b, ca, cb):
    return lax.dot_general(a, b, (((ca,), (cb,)), ((), ())), preferred_element_type=F32)


def attention_kernel(
    core_ref, q_ref, l2_ref, l1_ref, own_ref, r1_ref, r2_ref, fog_ref, low_ref, odp_ref, bias_ref,
    kept_ref, send_ref, dq_ref, pl2_ref, pl1_ref, pown_ref, pr1_ref, pr2_ref, attn_ref, kv_ref,
):
    part_refs = (pl2_ref, pl1_ref, pown_ref, pr1_ref, pr2_ref)
    rows, half = q_ref.shape
    for ref, (a, b) in zip((l2_ref, l1_ref, own_ref, r1_ref, r2_ref), SEGMENTS):
        kv_ref[a:b] = ref[...]
    window = kv_ref.shape[0]
    dout = (fog_ref[...].astype(F32) + STRENGTH * dot(low_ref[1][:, : odp_ref.shape[1]], odp_ref[...], 1, 1)).astype(BF)
    bias = bias_ref[...]
    for head in range(half // HDIM):
        cols = slice(head * HDIM, (head + 1) * HDIM)
        vcols = slice(half + head * HDIM, half + (head + 1) * HDIM)
        q, dout_h = q_ref[:, cols], dout[:, cols]
        k, v = kv_ref[:, cols], kv_ref[:, vcols]
        s = (dot(q, k, 1, 1) * SCALING).reshape(8, BLK, window)
        s = (s + bias[:, None, :]).reshape(rows, window)
        weights = jnp.exp(s - s.max(axis=1, keepdims=True))
        probs = weights * (1.0 / weights.sum(axis=1, keepdims=True))
        probs_low = probs.astype(BF)
        attn = dot(probs_low, v, 1, 0).astype(BF)
        attn_ref[:, cols] = attn
        delta = (dout_h.astype(F32) * attn.astype(F32)).sum(axis=1, keepdims=True)
        dscore = (probs * (dot(dout_h, v, 1, 1) - delta)).astype(BF)
        dq_ref[:, cols] = (dot(dscore, k, 1, 0) * SCALING).astype(BF)
        dk = dot(dscore, q, 0, 0) * SCALING
        dv = dot(probs_low, dout_h, 0, 0)
        for ref, (a, b) in zip(part_refs, SEGMENTS):
            ref[:, cols] = dk[a:b].astype(ref.dtype)
            ref[:, vcols] = dv[a:b].astype(ref.dtype)

    @pl.when(core_ref[0] == 0)
    def _():
        kept_ref[...] = dq_ref[...]
        send_ref[:rows] = attn_ref[...]

    @pl.when(core_ref[0] != 0)
    def _():
        kept_ref[...] = attn_ref[...]
        send_ref[:rows] = dq_ref[...]

    send_ref[rows:] = dq_ref[rows // 2 :]


def attention(core, q, windows, fog, low, odp_half, bias):
    rows, half = q.shape
    shape = jax.ShapeDtypeStruct
    outs = [shape((rows, half), BF), shape((rows + rows // 2, half), BF), shape((rows, half), BF)]
    outs += [shape((b - a, 2 * half), F32 if i == 2 else BF) for i, (a, b) in enumerate(SEGMENTS)]
    vmem = pl.BlockSpec(memory_space=pltpu.VMEM)
    return pl.pallas_call(
        attention_kernel,
        out_shape=outs,
        in_specs=[pl.BlockSpec(memory_space=pltpu.SMEM)] + [vmem] * 10,
        out_specs=[vmem] * 8,
        scratch_shapes=[pltpu.VMEM((rows, half), BF), pltpu.VMEM((SEGMENTS[-1][1], 2 * half), BF)],
        compiler_params=pltpu.CompilerParams(vmem_limit_bytes=40 * 1024 * 1024),
        cost_estimate=pl.CostEstimate(flops=700_000_000, bytes_accessed=4_000_000, transcendentals=524288),
        name="attention",
    )(core, q, *windows, fog, low, odp_half, bias)


Z_STEP = 4


def low_kernel(core_ref, xo_ref, xt_ref, yo_ref, yt_ref, w_ref, low_ref, own_acc, other_acc):
    core = core_ref[0]
    step = pl.program_id(0)
    rows = xo_ref.shape[0]
    ranks = w_ref.shape[3]
    block = NX * w_ref.shape[2]

    @pl.when(step == 0)
    def _():
        own_acc[...] = jnp.zeros_like(own_acc)
        other_acc[...] = jnp.zeros_like(other_acc)

    lane = lax.broadcasted_iota(jnp.int32, (rows, ranks), 1)
    from_y = (lane < ranks // 2) & (core == 1)
    for zz in range(Z_STEP):
        cols = slice(zz * block, (zz + 1) * block)
        w = jnp.concatenate([w_ref[i, zz] for i in range(NX)], axis=0)
        for x_ref, y_ref, acc in ((xo_ref, yo_ref, own_acc), (xt_ref, yt_ref, other_acc)):
            acc[...] += jnp.where(from_y, dot(y_ref[:, cols], w, 1, 0), dot(x_ref[:, cols], w, 1, 0))

    @pl.when(step == pl.num_programs(0) - 1)
    def _():
        low_ref[pl.ds(pl.multiple_of(core * rows, rows), rows)] = own_acc[...].astype(BF)
        low_ref[pl.ds(pl.multiple_of((1 - core) * rows, rows), rows)] = other_acc[...].astype(BF)


def low_factors(core, x_own, x_other, y_own, y_other, weights):
    rows, width = x_own.shape
    pieces, ranks = weights.shape[2:]
    wide = pl.BlockSpec((rows, width * Z_STEP // NZ), lambda i: (0, i))
    return pl.pallas_call(
        low_kernel,
        grid=(NZ // Z_STEP,),
        out_shape=jax.ShapeDtypeStruct((2 * rows, ranks), BF),
        in_specs=[pl.BlockSpec(memory_space=pltpu.SMEM)] + [wide] * 4
        + [pl.BlockSpec((NX, Z_STEP, pieces, ranks), lambda i: (0, i, 0, 0))],
        out_specs=pl.BlockSpec((2 * rows, ranks), lambda i: (0, 0)),
        scratch_shapes=[pltpu.VMEM((rows, ranks), F32), pltpu.VMEM((rows, ranks), F32)],
        compiler_params=pltpu.CompilerParams(vmem_limit_bytes=24 * 1024 * 1024),
        cost_estimate=pl.CostEstimate(flops=700_000_000, bytes_accessed=6_600_000, transcendentals=0),
        name="low_factors",
    )(core, x_own, x_other, y_own, y_other, weights)


def grad_kernel(
    scale, core_ref, xo_ref, xt_ref, yo_ref, yt_ref, kept_a_ref, got_a_ref, kept_b_ref, got_b_ref, low_ref,
    m_a_ref, m_b_ref, g_ref, f_ref, u_ref,
):
    core = core_ref[0]
    step = pl.program_id(0)
    rows = xo_ref.shape[0]
    half = kept_a_ref.shape[1]
    rank = m_a_ref.shape[1]
    block = xo_ref.shape[1] // Z_STEP
    piece = block // NX
    extra = g_ref.shape[2] - piece
    mine = pl.ds(pl.multiple_of(core * half, half), half)
    theirs = pl.ds(pl.multiple_of((1 - core) * half, half), half)

    @pl.when(step == 0)
    def _():
        for i, (kept_ref, got_ref, m_ref) in enumerate(
            ((kept_a_ref, got_a_ref, m_a_ref), (kept_b_ref, got_b_ref, m_b_ref))
        ):
            kept, got = kept_ref[...], got_ref[: 2 * rows]
            ranks = slice(i * rank, (i + 1) * rank)
            low = low_ref[:, ranks]
            f_ref[:, ranks] = (dot(kept, m_ref[mine], 1, 0) + dot(got, m_ref[theirs], 1, 0)).astype(BF)
            u_ref[ranks, mine] = (dot(low, kept, 0, 0) * scale).astype(BF)
            u_ref[ranks, theirs] = (dot(low, got, 0, 0) * scale).astype(BF)

    f_own = f_ref[pl.ds(pl.multiple_of(core * rows, rows), rows)]
    f_other = f_ref[pl.ds(pl.multiple_of((1 - core) * rows, rows), rows)]
    from_y = jnp.full((rank, block), core) == 1
    for zz in range(Z_STEP):
        cols = slice(zz * block, (zz + 1) * block)
        gx = dot(f_own, xo_ref[:, cols], 0, 0) + dot(f_other, xt_ref[:, cols], 0, 0)
        gy = dot(f_own[:, :rank], yo_ref[:, cols], 0, 0) + dot(f_other[:, :rank], yt_ref[:, cols], 0, 0)
        g = jnp.concatenate([jnp.where(from_y, gy, gx[:rank]), gx[rank:]], axis=0)
        g = (g * scale).T.astype(BF)
        at = pl.ds(pl.multiple_of((step * Z_STEP + zz) * extra, extra), extra)
        for i in range(NX):
            g_ref[i, zz, :piece] = g[i * piece : (i + 1) * piece]
            g_ref[i, zz, piece:] = u_ref[at, i * 2 * rank : (i + 1) * 2 * rank]


def grad_partials(scale, core, x_own, x_other, y_own, y_other, kept_a, got_a, kept_b, got_b, low, m_a, m_b):
    rows, width = x_own.shape
    feats, rank = m_a.shape
    piece = width // (NX * NZ)
    extra = 2 * rank // NZ
    wide = pl.BlockSpec((rows, width * Z_STEP // NZ), lambda i: (0, i))
    whole = [pl.BlockSpec(a.shape, lambda i: (0, 0)) for a in (kept_a, got_a, kept_b, got_b, low, m_a, m_b)]
    return pl.pallas_call(
        lambda *refs: grad_kernel(scale, *refs),
        grid=(NZ // Z_STEP,),
        out_shape=jax.ShapeDtypeStruct((NX, NZ, piece + extra, 2 * rank), BF),
        in_specs=[pl.BlockSpec(memory_space=pltpu.SMEM)] + [wide] * 4 + whole,
        out_specs=pl.BlockSpec((NX, Z_STEP, piece + extra, 2 * rank), lambda i: (0, i, 0, 0)),
        scratch_shapes=[pltpu.VMEM((2 * rows, 2 * rank), BF), pltpu.VMEM((2 * rank, feats), BF)],
        compiler_params=pltpu.CompilerParams(vmem_limit_bytes=24 * 1024 * 1024),
        cost_estimate=pl.CostEstimate(flops=800_000_000, bytes_accessed=7_500_000, transcendentals=0),
        name="grad_partials",
    )(core, x_own, x_other, y_own, y_other, kept_a, got_a, kept_b, got_b, low, m_a, m_b)


def exchange(parts, axes):
    return lax.all_to_all(parts, axes, split_axis=0, concat_axis=0, tiled=True)


def spread(block, axes, peers):
    return exchange(jnp.broadcast_to(block[None], (peers,) + block.shape), axes)


def swap(block):
    return lax.ppermute(block, "c", [(0, 1), (1, 0)])


def chip_shift(block, by):
    chips = NX * NY
    return lax.ppermute(block, ("x", "y"), [(i, i + by) for i in range(chips) if 0 <= i + by < chips])


def shards(
    inputs, queries, key_rows, values, frozen_output_gradient, out_grad, block_lists,
    down_qkv, up_qkv, output_down_projection, up_out,
):
    x_own, y_own = inputs[0], out_grad[0]
    rows, feats = queries.shape[1:]
    half = feats // 2
    rank = output_down_projection.shape[1]
    width = x_own.shape[1]
    own_cols = down_qkv.shape[1]
    core = lax.axis_index("c")
    first = core == 0
    chip = lax.axis_index("x") * NY + lax.axis_index("y")
    grad_scale = STRENGTH / math.sqrt(NX * NY * NZ * 2 * rows)

    core_id = core.astype(jnp.int32).reshape(1)

    shard = jnp.concatenate([down_qkv[0], down_qkv[1], up_out.T, down_qkv[2]], axis=1)
    copies = jnp.broadcast_to(shard.reshape(1, 2, -1), (2 * NY, 2, 2 * own_cols * rank))
    saved = (queries[0], frozen_output_gradient[0], key_rows[0], values[0])
    stack = jnp.concatenate(saved, axis=0)
    copies, stack = lax.optimization_barrier((copies, stack))
    line = exchange(copies, ("y", "c")).reshape(2 * NY * own_cols, 4 * rank)
    line = lax.dynamic_slice_in_dim(line, core * 2 * rank, 2 * rank, 1)

    lists = jnp.pad(block_lists[0].astype(BF), ((0, 12), (0, half - block_lists.shape[2])))
    kept = jnp.concatenate([jnp.where(first, stack[:, :half], stack[:, half:]), lists], axis=0)
    got = swap(jnp.concatenate([jnp.where(first, stack[:, half:], stack[:, :half]), lists], axis=0))
    chip_stack = jnp.stack([jnp.where(first, kept, got), jnp.where(first, got, kept)])
    line, chip_stack, x_own, y_own = lax.optimization_barrier((line, chip_stack, x_own, y_own))
    x_other = swap(x_own)
    y_other = lax.ppermute(y_own, "c", [(0, 1)])

    q_chip = chip_stack[:, :rows].reshape(2 * rows, half)
    fog_chip = chip_stack[:, rows : 2 * rows].reshape(2 * rows, half)
    kv_chip = jnp.concatenate(
        [chip_stack[:, 2 * rows : 3 * rows], chip_stack[:, 3 * rows : 4 * rows]], axis=2
    ).reshape(2 * rows, 2 * half)
    lists_chip = chip_stack[:, 4 * rows : 4 * rows + BLK_DEV, : block_lists.shape[2]].reshape(
        2 * BLK_DEV, -1
    )
    l1, r1 = chip_shift(kv_chip, 1), chip_shift(kv_chip, -1)
    ids = (2 * chip - 3) * BLK_DEV + jnp.arange(8 * BLK_DEV, dtype=jnp.int32)
    allowed = jnp.any(lists_chip[:, :, None] == ids.astype(F32)[None, None, :], axis=1) & (ids >= 0)[None]
    bias = jnp.repeat(jnp.where(allowed, 0.0, MASKED).astype(F32), BLK, axis=1)

    plane = spread(line, "z", NZ)
    copies = jnp.broadcast_to(plane.reshape(1, -1, 2 * rank), (NX, NZ * plane.shape[1], 2 * rank))
    m_a = jnp.where(first, up_qkv[0].T, output_down_projection)
    m_b = jnp.where(first, up_qkv[1].T, up_qkv[2].T)
    copies, kv_late, bias, m_a, m_b = lax.optimization_barrier((copies, kv_chip, bias, m_a, m_b))
    windows = (chip_shift(kv_late[rows:], 2), l1, kv_chip, r1, chip_shift(kv_late[:rows], -2))
    weights = exchange(copies, "x").reshape(NX, NZ, -1, 2 * rank)
    low = low_factors(core_id, x_own, x_other, y_own, y_other, weights)
    low_both = lax.all_gather(low, "c")
    odp_half = lax.dynamic_slice_in_dim(output_down_projection, core * half, half, 0)

    kept_a, send_a, dq, p_l2, p_l1, p_own, p_r1, p_r2 = attention(
        core_id, q_chip, windows, fog_chip, low_both, odp_half, bias
    )
    from_r1 = chip_shift(p_l1, -1)
    from_l1 = chip_shift(p_r1, 1)
    from_r2 = chip_shift(p_l2, -2)
    from_l2 = chip_shift(p_r2, 2)
    got_a = swap(send_a)

    total = p_own + from_r1.astype(F32) + from_l1.astype(F32)
    total = total + jnp.concatenate([from_l2, from_r2], axis=0).astype(F32)
    total = total.astype(BF)
    dk, dv = total[:, :half], total[:, half:]
    kept_b = jnp.where(first, dk, dv)
    got_b = swap(
        jnp.concatenate([jnp.where(first, dv, dk), jnp.where(first, dk[rows:], dv[:rows])], axis=0)
    )
    g = grad_partials(
        grad_scale, core_id, x_own, x_other, y_own, y_other, kept_a, got_a, kept_b, got_b, low, m_a, m_b
    )

    line_rows = 2 * NY * own_cols
    u_rows = g.shape[2] - line_rows
    step = exchange(g.reshape(NX, -1, 2 * rank), "x")
    step = step.astype(F32).sum(axis=0).astype(BF).reshape(NZ, -1, 2 * rank)
    step = exchange(step, "z")
    step = step.astype(F32).sum(axis=0).astype(BF)
    g_line = step[:line_rows].reshape(2 * NY, own_cols, 2 * rank)
    u_line = jnp.broadcast_to(step[line_rows:][None], (2 * NY, u_rows, 2 * rank))
    step = exchange(jnp.concatenate([g_line, u_line], axis=1), ("y", "c"))
    step = step.reshape(NY, 2, own_cols + u_rows, 2 * rank).astype(F32).sum(axis=0)
    g_out = step[:, :own_cols]
    grad_down = jnp.stack([g_out[0, :, :rank], g_out[0, :, rank:], g_out[1, :, rank:]])
    grad_up_out = g_out[1, :, :rank].T
    u_mine = step[:, own_cols:].astype(BF).reshape(2 * u_rows, 2 * rank)
    u_all = spread(u_mine, ("x", "z"), NX * NZ).reshape(NX, NZ, 2, u_rows, 2 * rank)
    u_all = jnp.transpose(u_all, (2, 1, 3, 0, 4)).reshape(2, 2, rank, feats).astype(F32)
    grad_up = jnp.stack([u_all[0, 0], u_all[0, 1], u_all[1, 1]])
    grad_down_out = u_all[1, 0].T

    def own_frame(mine, from_zero, from_one):
        left = jnp.where(first, mine[:rows], from_zero)
        right = jnp.where(first, from_one, mine[rows:])
        return jnp.concatenate([left, right], axis=1)[None]

    grad_q = own_frame(dq, got_a[2 * rows :], got_a[:rows])
    grad_k = own_frame(dk, got_b[2 * rows :], got_b[:rows])
    grad_v = own_frame(dv, got_b[rows : 2 * rows], got_b[2 * rows :])
    return grad_q, grad_k, grad_v, grad_down, grad_up, grad_down_out, grad_up_out


def solution(mesh):
    fine = Mesh(mesh.devices.reshape(NZ, NX, NY, 2), ("z", "x", "y", "c"))
    ctx = ("x", "y", "c")
    every = ("z", "x", "y", "c")
    tokens = P("z", ctx, None)
    return jax.shard_map(
        shards,
        mesh=fine,
        in_specs=(tokens,) * 7 + (P(None, every, None), P(), P(), P(None, every)),
        out_specs=(tokens,) * 3 + (P(None, every, None), P(), P(), P(None, every)),
        check_vma=False,
    )
```

```python
import math

import jax
import jax.numpy as jnp
from jax import lax
from jax.experimental import pallas as pl
from jax.experimental.pallas import tpu as pltpu
from jax.sharding import Mesh, PartitionSpec as P

HDIM = 128
BLK = 32
BLK_DEV = 4
NX, NY, NZ = 4, 8, 8
STRENGTH = 2.0
SCALING = HDIM**-0.5
MASKED = -1e30
BF = jnp.bfloat16
F32 = jnp.float32

SEGMENTS = ((0, 128), (128, 384), (384, 640), (640, 896), (896, 1024))


def dot(a, b, ca, cb):
    return lax.dot_general(a, b, (((ca,), (cb,)), ((), ())), preferred_element_type=F32)


def attention_kernel(
    core_ref, q_ref, l2_ref, l1_ref, own_ref, r1_ref, r2_ref, fog_ref, low_ref, odp_ref, bias_ref,
    kept_ref, send_ref, dq_ref, pl2_ref, pl1_ref, pown_ref, pr1_ref, pr2_ref, attn_ref, kv_ref,
):
    part_refs = (pl2_ref, pl1_ref, pown_ref, pr1_ref, pr2_ref)
    rows, half = q_ref.shape
    for ref, (a, b) in zip((l2_ref, l1_ref, own_ref, r1_ref, r2_ref), SEGMENTS):
        kv_ref[a:b] = ref[...]
    window = kv_ref.shape[0]
    dout = (fog_ref[...].astype(F32) + STRENGTH * dot(low_ref[1][:, : odp_ref.shape[1]], odp_ref[...], 1, 1)).astype(BF)
    bias = bias_ref[...]
    for head in range(half // HDIM):
        cols = slice(head * HDIM, (head + 1) * HDIM)
        vcols = slice(half + head * HDIM, half + (head + 1) * HDIM)
        q, dout_h = q_ref[:, cols], dout[:, cols]
        k, v = kv_ref[:, cols], kv_ref[:, vcols]
        s = (dot(q, k, 1, 1) * SCALING).reshape(8, BLK, window)
        s = (s + bias[:, None, :]).reshape(rows, window)
        weights = jnp.exp(s - s.max(axis=1, keepdims=True))
        probs = weights * (1.0 / weights.sum(axis=1, keepdims=True))
        probs_low = probs.astype(BF)
        attn = dot(probs_low, v, 1, 0).astype(BF)
        attn_ref[:, cols] = attn
        delta = (dout_h.astype(F32) * attn.astype(F32)).sum(axis=1, keepdims=True)
        dscore = (probs * (dot(dout_h, v, 1, 1) - delta)).astype(BF)
        dq_ref[:, cols] = (dot(dscore, k, 1, 0) * SCALING).astype(BF)
        dk = dot(dscore, q, 0, 0) * SCALING
        dv = dot(probs_low, dout_h, 0, 0)
        for ref, (a, b) in zip(part_refs, SEGMENTS):
            ref[:, cols] = dk[a:b].astype(ref.dtype)
            ref[:, vcols] = dv[a:b].astype(ref.dtype)

    @pl.when(core_ref[0] == 0)
    def _():
        kept_ref[...] = dq_ref[...]
        send_ref[:rows] = attn_ref[...]

    @pl.when(core_ref[0] != 0)
    def _():
        kept_ref[...] = attn_ref[...]
        send_ref[:rows] = dq_ref[...]

    send_ref[rows:] = dq_ref[rows // 2 :]


def attention(core, q, windows, fog, low, odp_half, bias):
    rows, half = q.shape
    shape = jax.ShapeDtypeStruct
    outs = [shape((rows, half), BF), shape((rows + rows // 2, half), BF), shape((rows, half), BF)]
    outs += [shape((b - a, 2 * half), F32 if i == 2 else BF) for i, (a, b) in enumerate(SEGMENTS)]
    vmem = pl.BlockSpec(memory_space=pltpu.VMEM)
    return pl.pallas_call(
        attention_kernel,
        out_shape=outs,
        in_specs=[pl.BlockSpec(memory_space=pltpu.SMEM)] + [vmem] * 10,
        out_specs=[vmem] * 8,
        scratch_shapes=[pltpu.VMEM((rows, half), BF), pltpu.VMEM((SEGMENTS[-1][1], 2 * half), BF)],
        compiler_params=pltpu.CompilerParams(vmem_limit_bytes=40 * 1024 * 1024),
        cost_estimate=pl.CostEstimate(flops=700_000_000, bytes_accessed=4_000_000, transcendentals=524288),
        name="attention",
    )(core, q, *windows, fog, low, odp_half, bias)


Z_STEP = 4


def low_kernel(core_ref, xo_ref, xt_ref, yo_ref, yt_ref, w_ref, low_ref, own_acc, other_acc):
    core = core_ref[0]
    step = pl.program_id(0)
    rows = xo_ref.shape[0]
    ranks = w_ref.shape[3]
    block = NX * w_ref.shape[2]

    @pl.when(step == 0)
    def _():
        own_acc[...] = jnp.zeros_like(own_acc)
        other_acc[...] = jnp.zeros_like(other_acc)

    lane = lax.broadcasted_iota(jnp.int32, (rows, ranks), 1)
    from_y = (lane < ranks // 2) & (core == 1)
    for zz in range(Z_STEP):
        cols = slice(zz * block, (zz + 1) * block)
        w = jnp.concatenate([w_ref[i, zz] for i in range(NX)], axis=0)
        for x_ref, y_ref, acc in ((xo_ref, yo_ref, own_acc), (xt_ref, yt_ref, other_acc)):
            acc[...] += jnp.where(from_y, dot(y_ref[:, cols], w, 1, 0), dot(x_ref[:, cols], w, 1, 0))

    @pl.when(step == pl.num_programs(0) - 1)
    def _():
        low_ref[pl.ds(pl.multiple_of(core * rows, rows), rows)] = own_acc[...].astype(BF)
        low_ref[pl.ds(pl.multiple_of((1 - core) * rows, rows), rows)] = other_acc[...].astype(BF)


def low_factors(core, x_own, x_other, y_own, y_other, weights):
    rows, width = x_own.shape
    pieces, ranks = weights.shape[2:]
    wide = pl.BlockSpec((rows, width * Z_STEP // NZ), lambda i: (0, i))
    return pl.pallas_call(
        low_kernel,
        grid=(NZ // Z_STEP,),
        out_shape=jax.ShapeDtypeStruct((2 * rows, ranks), BF),
        in_specs=[pl.BlockSpec(memory_space=pltpu.SMEM)] + [wide] * 4
        + [pl.BlockSpec((NX, Z_STEP, pieces, ranks), lambda i: (0, i, 0, 0))],
        out_specs=pl.BlockSpec((2 * rows, ranks), lambda i: (0, 0)),
        scratch_shapes=[pltpu.VMEM((rows, ranks), F32), pltpu.VMEM((rows, ranks), F32)],
        compiler_params=pltpu.CompilerParams(vmem_limit_bytes=24 * 1024 * 1024),
        cost_estimate=pl.CostEstimate(flops=700_000_000, bytes_accessed=6_600_000, transcendentals=0),
        name="low_factors",
    )(core, x_own, x_other, y_own, y_other, weights)


def grad_kernel(
    scale, core_ref, xo_ref, xt_ref, yo_ref, yt_ref, kept_a_ref, got_a_ref, kept_b_ref, got_b_ref, low_ref,
    m_a_ref, m_b_ref, g_ref, f_ref, u_ref,
):
    core = core_ref[0]
    step = pl.program_id(0)
    rows = xo_ref.shape[0]
    half = kept_a_ref.shape[1]
    rank = m_a_ref.shape[1]
    block = xo_ref.shape[1] // Z_STEP
    piece = block // NX
    extra = g_ref.shape[2] - piece
    mine = pl.ds(pl.multiple_of(core * half, half), half)
    theirs = pl.ds(pl.multiple_of((1 - core) * half, half), half)

    @pl.when(step == 0)
    def _():
        for i, (kept_ref, got_ref, m_ref) in enumerate(
            ((kept_a_ref, got_a_ref, m_a_ref), (kept_b_ref, got_b_ref, m_b_ref))
        ):
            kept, got = kept_ref[...], got_ref[: 2 * rows]
            ranks = slice(i * rank, (i + 1) * rank)
            low = low_ref[:, ranks]
            f_ref[:, ranks] = (dot(kept, m_ref[mine], 1, 0) + dot(got, m_ref[theirs], 1, 0)).astype(BF)
            u_ref[ranks, mine] = (dot(low, kept, 0, 0) * scale).astype(BF)
            u_ref[ranks, theirs] = (dot(low, got, 0, 0) * scale).astype(BF)

    f_own = f_ref[pl.ds(pl.multiple_of(core * rows, rows), rows)]
    f_other = f_ref[pl.ds(pl.multiple_of((1 - core) * rows, rows), rows)]
    from_y = jnp.full((rank, block), core) == 1
    for zz in range(Z_STEP):
        cols = slice(zz * block, (zz + 1) * block)
        gx = dot(f_own, xo_ref[:, cols], 0, 0) + dot(f_other, xt_ref[:, cols], 0, 0)
        gy = dot(f_own[:, :rank], yo_ref[:, cols], 0, 0) + dot(f_other[:, :rank], yt_ref[:, cols], 0, 0)
        g = jnp.concatenate([jnp.where(from_y, gy, gx[:rank]), gx[rank:]], axis=0)
        g = (g * scale).T.astype(BF)
        at = pl.ds(pl.multiple_of((step * Z_STEP + zz) * extra, extra), extra)
        for i in range(NX):
            g_ref[i, zz, :piece] = g[i * piece : (i + 1) * piece]
            g_ref[i, zz, piece:] = u_ref[at, i * 2 * rank : (i + 1) * 2 * rank]


def grad_partials(scale, core, x_own, x_other, y_own, y_other, kept_a, got_a, kept_b, got_b, low, m_a, m_b):
    rows, width = x_own.shape
    feats, rank = m_a.shape
    piece = width // (NX * NZ)
    extra = 2 * rank // NZ
    wide = pl.BlockSpec((rows, width * Z_STEP // NZ), lambda i: (0, i))
    whole = [pl.BlockSpec(a.shape, lambda i: (0, 0)) for a in (kept_a, got_a, kept_b, got_b, low, m_a, m_b)]
    return pl.pallas_call(
        lambda *refs: grad_kernel(scale, *refs),
        grid=(NZ // Z_STEP,),
        out_shape=jax.ShapeDtypeStruct((NX, NZ, piece + extra, 2 * rank), BF),
        in_specs=[pl.BlockSpec(memory_space=pltpu.SMEM)] + [wide] * 4 + whole,
        out_specs=pl.BlockSpec((NX, Z_STEP, piece + extra, 2 * rank), lambda i: (0, i, 0, 0)),
        scratch_shapes=[pltpu.VMEM((2 * rows, 2 * rank), BF), pltpu.VMEM((2 * rank, feats), BF)],
        compiler_params=pltpu.CompilerParams(vmem_limit_bytes=24 * 1024 * 1024),
        cost_estimate=pl.CostEstimate(flops=800_000_000, bytes_accessed=7_500_000, transcendentals=0),
        name="grad_partials",
    )(core, x_own, x_other, y_own, y_other, kept_a, got_a, kept_b, got_b, low, m_a, m_b)


def spread_out_kernel(u_ref, up_ref, down_ref):
    rank = down_ref.shape[0]
    rows, cols = u_ref.shape[3:]
    for core in range(2):
        for z in range(NZ):
            role, row = divmod(z * rows, rank)
            for x in range(NX):
                block = u_ref[x, z, core].astype(F32)
                at = (slice(row, row + rows), slice(x * cols, (x + 1) * cols))
                if core == 1 and role == 0:
                    down_ref[at] = block
                else:
                    up_ref[(core + role, *at)] = block


def spread_out(u_all, rank):
    feats = NX * u_all.shape[4]
    vmem = pl.BlockSpec(memory_space=pltpu.VMEM)
    return pl.pallas_call(
        spread_out_kernel,
        out_shape=[jax.ShapeDtypeStruct((3, rank, feats), F32), jax.ShapeDtypeStruct((rank, feats), F32)],
        in_specs=[vmem],
        out_specs=[vmem] * 2,
        compiler_params=pltpu.CompilerParams(vmem_limit_bytes=8 * 1024 * 1024),
        cost_estimate=pl.CostEstimate(flops=131072, bytes_accessed=786432, transcendentals=0),
        name="spread_out",
    )(u_all)


def exchange(parts, axes):
    return lax.all_to_all(parts, axes, split_axis=0, concat_axis=0, tiled=True)


def spread(block, axes, peers):
    return exchange(jnp.broadcast_to(block[None], (peers,) + block.shape), axes)


def swap(block):
    return lax.ppermute(block, "c", [(0, 1), (1, 0)])


def chip_shift(block, by):
    chips = NX * NY
    return lax.ppermute(block, ("x", "y"), [(i, i + by) for i in range(chips) if 0 <= i + by < chips])


def shards(
    inputs, queries, key_rows, values, frozen_output_gradient, out_grad, block_lists,
    down_qkv, up_qkv, output_down_projection, up_out,
):
    x_own, y_own = inputs[0], out_grad[0]
    rows, feats = queries.shape[1:]
    half = feats // 2
    rank = output_down_projection.shape[1]
    width = x_own.shape[1]
    own_cols = down_qkv.shape[1]
    core = lax.axis_index("c")
    first = core == 0
    chip = lax.axis_index("x") * NY + lax.axis_index("y")
    grad_scale = STRENGTH / math.sqrt(NX * NY * NZ * 2 * rows)

    core_id = core.astype(jnp.int32).reshape(1)

    shard = jnp.concatenate([down_qkv[0], down_qkv[1], up_out.T, down_qkv[2]], axis=1)
    copies = jnp.broadcast_to(shard.reshape(1, 2, -1), (2 * NY, 2, 2 * own_cols * rank))
    saved = (queries[0], frozen_output_gradient[0], key_rows[0], values[0])
    stack = jnp.concatenate(saved, axis=0)
    copies, stack = lax.optimization_barrier((copies, stack))
    line = exchange(copies, ("y", "c")).reshape(2 * NY * own_cols, 4 * rank)
    line = lax.dynamic_slice_in_dim(line, core * 2 * rank, 2 * rank, 1)

    lists = jnp.pad(block_lists[0].astype(BF), ((0, 12), (0, half - block_lists.shape[2])))
    kept = jnp.concatenate([jnp.where(first, stack[:, :half], stack[:, half:]), lists], axis=0)
    got = swap(jnp.concatenate([jnp.where(first, stack[:, half:], stack[:, :half]), lists], axis=0))
    chip_stack = jnp.stack([jnp.where(first, kept, got), jnp.where(first, got, kept)])
    line, chip_stack, x_own, y_own = lax.optimization_barrier((line, chip_stack, x_own, y_own))
    x_other = swap(x_own)
    y_other = lax.ppermute(y_own, "c", [(0, 1)])

    q_chip = chip_stack[:, :rows].reshape(2 * rows, half)
    fog_chip = chip_stack[:, rows : 2 * rows].reshape(2 * rows, half)
    kv_chip = jnp.concatenate(
        [chip_stack[:, 2 * rows : 3 * rows], chip_stack[:, 3 * rows : 4 * rows]], axis=2
    ).reshape(2 * rows, 2 * half)
    lists_chip = chip_stack[:, 4 * rows : 4 * rows + BLK_DEV, : block_lists.shape[2]].reshape(
        2 * BLK_DEV, -1
    )
    l1, r1 = chip_shift(kv_chip, 1), chip_shift(kv_chip, -1)
    ids = (2 * chip - 3) * BLK_DEV + jnp.arange(8 * BLK_DEV, dtype=jnp.int32)
    allowed = jnp.any(lists_chip[:, :, None] == ids.astype(F32)[None, None, :], axis=1) & (ids >= 0)[None]
    bias = jnp.repeat(jnp.where(allowed, 0.0, MASKED).astype(F32), BLK, axis=1)

    plane = spread(line, "z", NZ)
    copies = jnp.broadcast_to(plane.reshape(1, -1, 2 * rank), (NX, NZ * plane.shape[1], 2 * rank))
    m_a = jnp.where(first, up_qkv[0].T, output_down_projection)
    m_b = jnp.where(first, up_qkv[1].T, up_qkv[2].T)
    copies, kv_late, bias, m_a, m_b = lax.optimization_barrier((copies, kv_chip, bias, m_a, m_b))
    windows = (chip_shift(kv_late[rows:], 2), l1, kv_chip, r1, chip_shift(kv_late[:rows], -2))
    weights = exchange(copies, "x").reshape(NX, NZ, -1, 2 * rank)
    low = low_factors(core_id, x_own, x_other, y_own, y_other, weights)
    low_both = lax.all_gather(low, "c")
    odp_half = lax.dynamic_slice_in_dim(output_down_projection, core * half, half, 0)

    kept_a, send_a, dq, p_l2, p_l1, p_own, p_r1, p_r2 = attention(
        core_id, q_chip, windows, fog_chip, low_both, odp_half, bias
    )
    from_r1 = chip_shift(p_l1, -1)
    from_l1 = chip_shift(p_r1, 1)
    from_r2 = chip_shift(p_l2, -2)
    from_l2 = chip_shift(p_r2, 2)
    got_a = swap(send_a)

    total = p_own + from_r1.astype(F32) + from_l1.astype(F32)
    total = total + jnp.concatenate([from_l2, from_r2], axis=0).astype(F32)
    total = total.astype(BF)
    dk, dv = total[:, :half], total[:, half:]
    kept_b = jnp.where(first, dk, dv)
    got_b = swap(
        jnp.concatenate([jnp.where(first, dv, dk), jnp.where(first, dk[rows:], dv[:rows])], axis=0)
    )
    g = grad_partials(
        grad_scale, core_id, x_own, x_other, y_own, y_other, kept_a, got_a, kept_b, got_b, low, m_a, m_b
    )

    line_rows = 2 * NY * own_cols
    u_rows = g.shape[2] - line_rows
    step = exchange(g.reshape(NX, -1, 2 * rank), "x")
    step = step.astype(F32).sum(axis=0).astype(BF).reshape(NZ, -1, 2 * rank)
    step = exchange(step, "z")
    step = step.astype(F32).sum(axis=0).astype(BF)
    g_line = step[:line_rows].reshape(2 * NY, own_cols, 2 * rank)
    u_line = jnp.broadcast_to(step[line_rows:][None], (2 * NY, u_rows, 2 * rank))
    step = exchange(jnp.concatenate([g_line, u_line], axis=1), ("y", "c"))
    step = step.reshape(NY, 2, own_cols + u_rows, 2 * rank).astype(F32).sum(axis=0)
    g_out = step[:, :own_cols]
    grad_down = jnp.stack([g_out[0, :, :rank], g_out[0, :, rank:], g_out[1, :, rank:]])
    grad_up_out = g_out[1, :, :rank].T
    u_mine = step[:, own_cols:].astype(BF).reshape(2 * u_rows, 2 * rank)
    u_all = spread(u_mine, ("x", "z"), NX * NZ).reshape(NX, NZ, 2, u_rows, 2 * rank)
    grad_up, down_turned = spread_out(u_all, rank)
    grad_down_out = down_turned.T

    def own_frame(mine, from_zero, from_one):
        left = jnp.where(first, mine[:rows], from_zero)
        right = jnp.where(first, from_one, mine[rows:])
        return jnp.concatenate([left, right], axis=1)[None]

    grad_q = own_frame(dq, got_a[2 * rows :], got_a[:rows])
    grad_k = own_frame(dk, got_b[2 * rows :], got_b[:rows])
    grad_v = own_frame(dv, got_b[rows : 2 * rows], got_b[2 * rows :])
    return grad_q, grad_k, grad_v, grad_down, grad_up, grad_down_out, grad_up_out


def solution(mesh):
    fine = Mesh(mesh.devices.reshape(NZ, NX, NY, 2), ("z", "x", "y", "c"))
    ctx = ("x", "y", "c")
    every = ("z", "x", "y", "c")
    tokens = P("z", ctx, None)
    return jax.shard_map(
        shards,
        mesh=fine,
        in_specs=(tokens,) * 7 + (P(None, every, None), P(), P(), P(None, every)),
        out_specs=(tokens,) * 3 + (P(None, every, None), P(), P(), P(None, every)),
        check_vma=False,
    )
```
